512 devices in a mesh: lat: 32 (over z, x), lon: 16 (over y, core).
Axes of the slice: x: 4, y: 8, z: 8, core: 2. Of those that a mesh axis runs over, the one named last changes fastest.
Arguments:
- grid_field: bfloat16 [384, 768, 384], P('lat', 'lon'), may hold values from -6 to 6
- disco_filter: float32 [3, 5, 384], P(None, None, 'lat'), may hold values from -3 to 3
- offsets: int32 [3, 5, 384], P(None, None, 'lat'), may hold values from -2 to 2
- disco_weight: bfloat16 [3, 384, 384], replicated, may hold values from -0.1875 to 0.1875
- legendre: bfloat16 [2, 192, 384, 384], P(None, 'lat', None, 'lon'), as said below
- spec_weight: bfloat16 [2, 384, 384], replicated, may hold values from -0.21875 to 0.21875
- degree_gain: float32 [384, 384], replicated, may hold values from 0.25 to 2.5
Outputs:
- result: bfloat16 [384, 768, 384], P('lat', 'lon')
The draws below stay inside these ranges and needn't reach their ends.
Inputs may be any that keep to these rules, and one draw needn't show every extreme that they name: legendre[h, p, l, t] is zero wherever the degree l is below the entry's wavenumber (p for h = 0, 383 - p for h = 1).
All inputs are finite; a program needn't handle non-finite values.
Results may differ from the reference program's by a relative error of at most 0.0055.
Values may be sent and summed in bfloat16 or wider, within the bound.
A program may use at most 128 MiB of HBM per device.

```python
import math
import jax
import jax.numpy as jnp

C = 384
NLAT = 384
NLON = 768
MMAX = 384
LMAX = 384
KERNELS = 3


def draw_legendre(key, part):
    key = jax.random.fold_in(key, 11)
    pair_index = jnp.arange(MMAX // 2, dtype=jnp.int32)
    halves = jnp.arange(2, dtype=jnp.int32)
    wavenumber = jnp.where(halves[:, None] == 0, pair_index[None, :], MMAX - 1 - pair_index[None, :])
    degrees = jnp.arange(LMAX, dtype=jnp.int32)
    present = (degrees[None, None, :] >= wavenumber[:, :, None]).astype(jnp.float32)
    shape_all = (2, MMAX // 2, LMAX, NLAT)
    values = jax.random.normal(key, shape_all, jnp.float32)
    values = values * present[..., None] / math.sqrt(NLAT)
    return values.astype(jnp.bfloat16)


def plant(array, key, low, largest):
    shape = array.shape
    place = [jax.random.randint(jax.random.fold_in(key, axis), (), 0, shape[axis]) for axis in range(len(shape))]
    array = array.at[tuple(place)].set(low)
    longest = shape.index(max(shape))
    place[longest] = (place[longest] + 1) % shape[longest]
    return array.at[tuple(place)].set(largest)


def shard_levels(rng, shape, shards, low, high):
    level = 1.0
    for axis_at, blocks in shards:
        steps = jax.random.uniform(jax.random.fold_in(jax.random.fold_in(rng, 6), axis_at), (blocks,), jnp.float32, low / len(shards), high / len(shards))
        level = level * jnp.repeat(jnp.exp(steps), shape[axis_at] // blocks).reshape((-1,) + (1,) * (len(shape) - 1 - axis_at))
    return level


def normal_values(own_key, shape, spread, limit, split=(), kind=jnp.bfloat16):
    gain = shard_levels(own_key, shape, split, -0.22, 0.18) if split else 1.0
    drawn = jax.random.normal(own_key, shape, jnp.float32) * spread * gain
    return jnp.minimum(jnp.maximum(drawn, -limit), limit).astype(kind)


def setup_inputs(seed: int = 0) -> dict:
    key_list = jax.random.split(jax.random.key(seed), 8)
    grid_field = normal_values(key_list[0], (NLAT, NLON, C), 1.0, 6.0, ((0, 32), (1, 16)))
    disco_filter = normal_values(key_list[1], (KERNELS, 5, NLAT), 0.5, 3.0, ((2, 32),), jnp.float32)
    offsets = plant(jax.random.randint(key_list[2], (KERNELS, 5, NLAT), -2, 3), jax.random.fold_in(key_list[2], 1), -2, 2).astype(jnp.int32)
    disco_weight = normal_values(key_list[3], (KERNELS, C, C), (KERNELS * C) ** -0.5, 0.1875)
    legendre = draw_legendre(jax.random.fold_in(key_list[7], 71), 0)
    spec_weight = normal_values(key_list[5], (2, C, C), (2 * C) ** -0.5, 0.21875)
    degree_gain = jnp.clip(jnp.exp(jax.random.uniform(key_list[6], (LMAX, C), jnp.float32, math.log(0.25), math.log(2.5))), 0.25, 2.5)
    return {"grid_field": grid_field, "disco_filter": disco_filter, "offsets": offsets, "disco_weight": disco_weight, "legendre": legendre, "spec_weight": spec_weight, "degree_gain": degree_gain}


def fourier_table(nlon, mmax):
    columns = jnp.arange(2 * mmax, dtype=jnp.int32)
    pair_index = columns // 4
    halves = columns // 2 % 2
    component = columns % 2
    wavenumber = jnp.where(halves == 0, pair_index, mmax - 1 - pair_index)
    longitude = jnp.arange(nlon, dtype=jnp.int32)
    phases = longitude[:, None] * wavenumber[None, :] % nlon
    angles = phases.astype(jnp.float32) * (2.0 * math.pi / nlon)
    norm_scale = 1.0 / math.sqrt(nlon)
    values = jnp.where(component[None, :] == 0, jnp.cos(angles), -jnp.sin(angles)) * norm_scale
    return values.astype(jnp.bfloat16)

def reference(grid_field, disco_filter, offsets, disco_weight, legendre, spec_weight, degree_gain):
    widened = jnp.concatenate([grid_field[:, -2:], grid_field, grid_field[:, :2]], axis=1)
    padded = jnp.pad(widened, ((2, 2), (0, 0), (0, 0)))
    disco = jnp.zeros((NLAT * NLON, C), jnp.float32)
    for basis in range(KERNELS):
        summed = jnp.zeros((NLAT, NLON, C), jnp.float32)
        for row_step in range(5):
            for col_step in range(5):
                row_coeff = jnp.where(offsets[basis, row_step] == col_step - 2, disco_filter[basis, row_step], 0.0)
                shifted = padded[row_step:row_step + NLAT, col_step:col_step + NLON].astype(jnp.float32)
                summed = summed + row_coeff[:, None, None] * shifted
        term = summed.astype(jnp.bfloat16).reshape(NLAT * NLON, C)
        disco = disco + jnp.dot(term.astype(jnp.float32), disco_weight[basis].astype(jnp.float32))
    disco = disco.reshape(NLAT, NLON, C)
    trig_table = fourier_table(NLON, MMAX).astype(jnp.float32)
    fourier = jnp.einsum('lnc,nk->lkc', grid_field.astype(jnp.float32), trig_table).astype(jnp.bfloat16)
    fourier = fourier.reshape(NLAT, MMAX // 2, 2, 2, C)
    table_wide = legendre.astype(jnp.float32)
    spectrum = jnp.einsum('hilt,tihrc->ihlrc', table_wide, fourier.astype(jnp.float32)).astype(jnp.bfloat16)
    w_real = spec_weight[0].astype(jnp.float32)
    w_imag = spec_weight[1].astype(jnp.float32)
    stacked_weight = jnp.concatenate([jnp.concatenate([w_real, w_imag], axis=1), jnp.concatenate([-w_imag, w_real], axis=1)], axis=0)
    flattened = spectrum.astype(jnp.float32).reshape(-1, 2 * C)
    mixed_rows = jnp.dot(flattened, stacked_weight).reshape(MMAX // 2, 2, LMAX, 2, C)
    filtered = (mixed_rows * degree_gain[None, None, :, None, :]).astype(jnp.bfloat16)
    returned = jnp.einsum('hilt,ihlrc->tihrc', table_wide, filtered.astype(jnp.float32)).astype(jnp.bfloat16)
    returned = returned.reshape(NLAT, 2 * MMAX, C)
    spectral = jnp.einsum('lkc,nk->lnc', returned.astype(jnp.float32), trig_table).astype(jnp.bfloat16)
    combined = spectral.astype(jnp.float32) + disco
    return (grid_field.astype(jnp.float32) + jax.nn.gelu(combined)).astype(jnp.bfloat16)
```

```python
import math

import jax
import jax.numpy as jnp
import numpy as np
from jax import lax
from jax.experimental import pallas as pl
from jax.experimental.pallas import tpu as pltpu
from jax.sharding import PartitionSpec as P

C = 384
NLAT = 384
NLON = 768
MMAX = 384
LMAX = 384
KERNELS = 3
LAT = 32
LON = 16
BAND = NLAT // LAT
TILE = NLON // LON
MS = 12
LEG = NLAT // LON
CHUNKS = 3
CW = C // CHUNKS
MESH = pl.DeviceIdType.MESH


def constant_tables():
    group = np.arange(LAT)[:, None, None, None]
    half = np.arange(2)[None, :, None, None]
    pair = np.arange(6)[None, None, :, None]
    index = group * 6 + pair
    wavenumber = np.where(half == 0, index, MMAX - 1 - index) + np.zeros((1, 1, 1, 2), np.int64)
    component = np.zeros_like(wavenumber) + np.arange(2)
    wavenumber = wavenumber.reshape(-1)
    component = component.reshape(-1)
    phases = (wavenumber[:, None] * np.arange(NLON)[None, :]) % NLON
    angles = phases.astype(np.float32) * np.float32(2.0 * math.pi / NLON)
    values = np.where(component[:, None] == 0, np.cos(angles), -np.sin(angles))
    values = values.astype(np.float32) * np.float32(1.0 / math.sqrt(NLON))
    table = jnp.asarray(values, jnp.bfloat16)
    table_t = jnp.asarray(values.T.copy(), jnp.bfloat16)
    perm = np.zeros((2 * MMAX, 2 * MMAX), np.float32)
    for band in range(LAT):
        for inner in range(2 * MS):
            perm[inner * LAT + band, band * 2 * MS + inner] = 1.0
    perm_leg = np.zeros((NLAT, NLAT), np.float32)
    for t in range(NLAT):
        perm_leg[(t % BAND) * LAT + t // BAND, t] = 1.0
    return (
        table,
        table_t,
        jnp.asarray(perm, jnp.bfloat16),
        jnp.asarray(perm.T.copy(), jnp.bfloat16),
        jnp.asarray(perm_leg, jnp.bfloat16),
    )


def dot(a, b):
    return jnp.dot(a, b, preferred_element_type=jnp.float32)


def kernel(
    grid_hbm, filt, offs, dw_hbm, leg_hbm, sw_hbm, gain_hbm, tab_hbm, tabt_hbm, pf_hbm, pb_hbm, pl_hbm,
    out_ref,
    grid_v, pad, dw, sw, gain, tab, tabt, pf, pb, pleg,
    legrecv, legp, legn, rows, fsend, frecv, gsend, hrecv, spec, rsend, gback, bsend, ret, ssend, srecv,
    basis, disco,
    load_sem, x1_send, x1_recv, leg_send, leg_recv, halo_send, halo_recv,
    a_send, a_recv, b_send, b_recv, c_send, c_recv, d_send, d_recv, e_send, e_recv,
):
    bf16 = jnp.bfloat16
    f32 = jnp.float32
    lat = lax.axis_index("lat")
    lon = lax.axis_index("lon")
    quad = lax.div(lon, 4)
    place = lax.rem(lon, 4)
    active = place < 3
    mine = quad * 3 + jnp.minimum(place, 2)

    north = lax.rem(lat + LAT - 1, LAT)
    south = lax.rem(lat + 1, LAT)
    west = lax.rem(lon + LON - 1, LON)
    east = lax.rem(lon + 1, LON)

    loads = [
        pltpu.make_async_copy(src, dst, load_sem.at[n])
        for n, (src, dst) in enumerate(
            (
                (grid_hbm, grid_v), (tab_hbm, tab), (pf_hbm, pf), (pl_hbm, pleg),
                (dw_hbm, dw), (sw_hbm, sw), (gain_hbm, gain), (pb_hbm, pb), (tabt_hbm, tabt),
            )
        )
    ]
    load_grid, load_tab, load_pf, load_pleg, load_dw, load_sw, load_gain, load_pb, load_tabt = loads
    for load in loads:
        load.start()

    barrier = pltpu.get_barrier_semaphore()

    def greet(device):
        pl.semaphore_signal(barrier, inc=1, device_id=device, device_id_type=MESH)

    @pl.loop(1, LON)
    def _(d):
        greet((lat, lax.rem(lon + d, LON)))

    @pl.loop(1, LAT)
    def _(d):
        greet((lax.rem(lat + d, LAT), lon))

    for a in (north, south):
        for b in (west, east):
            greet((a, b))
    pl.semaphore_wait(barrier, LON - 1 + LAT - 1 + 4)

    def owner(row):
        return row + lax.div(row, 3)

    def remote(src, dst, send, recv, device):
        return pltpu.make_async_remote_copy(
            src_ref=src, dst_ref=dst, send_sem=send, recv_sem=recv, device_id=device, device_id_type=MESH
        )

    def to_rows(source, target, send, recv):
        @pl.loop(0, BAND)
        def _(d):
            row = lax.rem(mine + d, BAND)
            there = owner(row)

            @pl.when(there != lon)
            def _():
                remote(source(row), target, send, recv, (lat, there)).start()

            @pl.when(there == lon)
            def _():
                pltpu.make_async_copy(source(row), target, recv).start()

    def to_bands(source, target, send, recv):
        @pl.loop(1, LAT)
        def _(d):
            there = lax.rem(lat + d, LAT)
            remote(source(there), target, send, recv, (there, lon)).start()

        pltpu.make_async_copy(source(lat), target, recv).start()

    def wait(ref, sem):
        pltpu.make_async_copy(ref, ref, sem).wait()

    for ch in range(CHUNKS):
        to_rows(
            lambda row: grid_hbm.at[row, :, pl.ds(ch * CW, CW)], rows.at[ch, lon], x1_send, x1_recv.at[ch]
        )

    load_grid.wait()
    for ct in range(C // 128):
        pad[ct, 2 : 2 + BAND, 8 : 8 + TILE, :] = grid_v[:, :, ct * 128 : (ct + 1) * 128].astype(f32)
    n0, n1 = 8, 8 + TILE
    t0, t1 = 2, 2 + BAND
    halo = [
        remote(
            pad.at[:, pl.ds(sr, nr), pl.ds(sc, nc), :], pad.at[:, pl.ds(dr, nr), pl.ds(dc, nc), :],
            halo_send.at[n], halo_recv.at[n], device,
        )
        for n, (sr, nr, sc, nc, dr, dc, device) in enumerate(
            (
                (t0, BAND, n0, 8, t0, n1, (lat, west)),
                (t0, BAND, n1 - 8, 8, t0, 0, (lat, east)),
                (t0, 2, n0, TILE, t1, n0, (north, lon)),
                (t1 - 2, 2, n0, TILE, 0, n0, (south, lon)),
                (t0, 2, n0, 8, t1, n1, (north, west)),
                (t0, 2, n1 - 8, 8, t1, 0, (north, east)),
                (t1 - 2, 2, n0, 8, 0, n1, (south, west)),
                (t1 - 2, 2, n1 - 8, 8, 0, 0, (south, east)),
            )
        )
    ]
    for copy in halo:
        copy.start()

    to_rows(lambda row: leg_hbm.at[row], legrecv.at[lon], leg_send, leg_recv)

    load_tab.wait()
    load_pf.wait()
    load_pleg.wait()

    @pl.when(active)
    def _():
        for ch in range(CHUNKS):
            wait(rows.at[ch], x1_recv.at[ch])

            @pl.loop(0, 4)
            def _(b):
                part = dot(tab[pl.ds(b * 192, 192), :], rows[ch].reshape(NLON, CW))
                fsend[ch, pl.ds(b * 8, 8)] = part.reshape(8, 2 * MS, CW).astype(bf16)

            to_bands(lambda q: fsend.at[ch, q], frecv.at[ch, lat], a_send, a_recv.at[ch])

        wait(legrecv, leg_recv)
        shards = legrecv[...].astype(f32).reshape(NLAT, LMAX).astype(bf16)
        ordered = dot(pleg[...], shards)
        legp[...] = ordered.astype(bf16)
        legn[...] = ordered.T.astype(bf16)

        for ch in range(CHUNKS):
            wait(frecv.at[ch], a_recv.at[ch])

            @pl.loop(0, 4)
            def _(b):
                got = frecv[ch].astype(f32).reshape(2 * MMAX, CW).astype(bf16)
                part = dot(pf[pl.ds(b * 192, 192), :], got)
                gsend[ch, pl.ds(b * 3, 3)] = part.reshape(3, 2 * LAT, CW).astype(bf16)

            to_rows(lambda m: gsend.at[ch, m], hrecv.at[ch, mine], b_send, b_recv.at[ch])

    load_dw.wait()
    for copy in halo:
        copy.wait_recv()

    @pl.loop(0, BAND)
    def _(i):
        for k in range(KERNELS):
            totals = [jnp.zeros((TILE, 128), f32)] * (C // 128)
            for j in range(5):
                t = lat * BAND + i + (j - 2)
                inside = jnp.logical_and(t >= 0, t < NLAT)
                scale = jnp.where(inside, filt[k, j, i], 0.0)
                first = 8 + offs[k, j, i]
                totals = [
                    total + scale * pad[ct, i + j, pl.ds(first, TILE), :] for ct, total in enumerate(totals)
                ]
            for ct, total in enumerate(totals):
                at = k * C + ct * 128
                basis[pl.ds(i * TILE, TILE), at : at + 128] = total.astype(bf16)

    @pl.loop(0, 4)
    def _(b):
        disco[pl.ds(b * 144, 144), :] = dot(basis[pl.ds(b * 144, 144), :], dw[...])

    load_sw.wait()
    load_gain.wait()
    load_pb.wait()
    load_tabt.wait()

    @pl.when(active)
    def _():
        for ch in range(CHUNKS):
            wait(hrecv.at[ch], b_recv.at[ch])
            for r in range(2):
                part = hrecv[ch, :, r * LAT : (r + 1) * LAT, :].reshape(NLAT, CW)
                spec[:, r * C + ch * CW : r * C + (ch + 1) * CW] = dot(legn[...], part).astype(bf16)

        for ch in range(CHUNKS):
            cols = slice(ch * CW, (ch + 1) * CW)
            re = spec[:, :C]
            im = spec[:, C:]
            filtered = (
                dot(re, sw[0, :, cols]) - dot(im, sw[1, :, cols]),
                dot(re, sw[1, :, cols]) + dot(im, sw[0, :, cols]),
            )
            for r in range(2):
                value = (filtered[r] * gain[:, cols]).astype(bf16)
                back = dot(legp[...], value)
                rsend[ch, :, r * LAT : (r + 1) * LAT, :] = back.astype(bf16).reshape(BAND, LAT, CW)
            to_rows(lambda row: rsend.at[ch, row], gback.at[ch, mine], c_send, c_recv.at[ch])

        for ch in range(CHUNKS):
            wait(gback.at[ch], c_recv.at[ch])

            @pl.loop(0, 4)
            def _(b):
                part = dot(pb[pl.ds(b * 192, 192), :], gback[ch].reshape(2 * MMAX, CW))
                bsend[ch, pl.ds(b * 8, 8)] = part.reshape(8, 2 * MS, CW).astype(bf16)

            to_bands(lambda q: bsend.at[ch, q], ret.at[ch, lat], d_send, d_recv.at[ch])

        for ch in range(CHUNKS):
            wait(ret.at[ch], d_recv.at[ch])

            @pl.loop(0, 4)
            def _(b):
                got = ret[ch].astype(f32).reshape(2 * MMAX, CW).astype(bf16)
                part = dot(tabt[pl.ds(b * 192, 192), :], got)
                ssend[ch, pl.ds(b * 4, 4)] = part.reshape(4, TILE, CW).astype(bf16)

            @pl.loop(1, LON)
            def _(d):
                there = lax.rem(lon + d, LON)
                remote(
                    ssend.at[ch, there], srecv.at[ch, mine], e_send, e_recv.at[ch], (lat, there)
                ).start()

            pltpu.make_async_copy(ssend.at[ch, lon], srecv.at[ch, mine], e_recv.at[ch]).start()

    for ch in range(CHUNKS):
        cols = slice(ch * CW, (ch + 1) * CW)
        wait(srecv.at[ch], e_recv.at[ch])

        @pl.loop(0, BAND)
        def _(i):
            combined = srecv[ch, i].astype(f32) + disco[pl.ds(i * TILE, TILE), cols]
            out_ref[i, :, cols] = (grid_v[i, :, cols].astype(f32) + jax.nn.gelu(combined)).astype(bf16)

    for copy in halo:
        copy.wait_send()

    @pl.when(active)
    def _():
        wait(rows.at[:, pl.ds(0, BAND - 1)], x1_send)
        wait(legrecv.at[pl.ds(0, MS - 1)], leg_send)
        wait(fsend.at[:, pl.ds(0, LAT - 1)], a_send)
        wait(gsend.at[:, pl.ds(0, MS - 1)], b_send)
        wait(rsend.at[:, pl.ds(0, BAND - 1)], c_send)
        wait(bsend.at[:, pl.ds(0, LAT - 1)], d_send)
        wait(ssend.at[:, pl.ds(0, LON - 1)], e_send)

    @pl.when(jnp.logical_not(active))
    def _():
        wait(rows.at[:, pl.ds(0, BAND)], x1_send)
        wait(legrecv.at[pl.ds(0, MS)], leg_send)


def on_device(grid_field, disco_filter, offsets, disco_weight, legendre, spec_weight, degree_gain):
    bf16 = jnp.bfloat16
    f32 = jnp.float32
    smem = pl.BlockSpec(memory_space=pltpu.SMEM)
    hbm = pl.BlockSpec(memory_space=pl.ANY)
    dma = pltpu.SemaphoreType.DMA
    vmem = pltpu.VMEM
    return pl.pallas_call(
        kernel,
        out_shape=jax.ShapeDtypeStruct(grid_field.shape, bf16),
        in_specs=[hbm, smem, smem] + [hbm] * 9,
        out_specs=pl.BlockSpec(memory_space=pltpu.VMEM),
        scratch_shapes=[
            vmem((BAND, TILE, C), bf16),
            vmem((C // 128, BAND + 4, TILE + 16, 128), f32),
            vmem((KERNELS * C, C), bf16),
            vmem((2, C, C), bf16),
            vmem((LMAX, C), f32),
            vmem((2 * MMAX, NLON), bf16),
            vmem((NLON, 2 * MMAX), bf16),
            vmem((2 * MMAX, 2 * MMAX), bf16),
            vmem((2 * MMAX, 2 * MMAX), bf16),
            vmem((NLAT, NLAT), bf16),
            vmem((LON, LEG, LMAX), bf16),
            vmem((NLAT, LMAX), bf16),
            vmem((LMAX, NLAT), bf16),
            vmem((CHUNKS, LON, TILE, CW), bf16),
            vmem((CHUNKS, LAT, 2 * MS, CW), bf16),
            vmem((CHUNKS, LAT, 2 * MS, CW), bf16),
            vmem((CHUNKS, MS, 2 * LAT, CW), bf16),
            vmem((CHUNKS, BAND, 2 * LAT, CW), bf16),
            vmem((LMAX, 2 * C), bf16),
            vmem((CHUNKS, BAND, 2 * LAT, CW), bf16),
            vmem((CHUNKS, MS, 2 * LAT, CW), bf16),
            vmem((CHUNKS, LAT, 2 * MS, CW), bf16),
            vmem((CHUNKS, LAT, 2 * MS, CW), bf16),
            vmem((CHUNKS, LON, TILE, CW), bf16),
            vmem((CHUNKS, BAND, TILE, CW), bf16),
            vmem((BAND * TILE, KERNELS * C), bf16),
            vmem((BAND * TILE, C), f32),
            dma((9,)),
            dma, dma((CHUNKS,)),
            dma, dma,
            dma((8,)), dma((8,)),
            dma, dma((CHUNKS,)),
            dma, dma((CHUNKS,)),
            dma, dma((CHUNKS,)),
            dma, dma((CHUNKS,)),
            dma, dma((CHUNKS,)),
        ],
        compiler_params=pltpu.CompilerParams(
            collective_id=0, has_side_effects=True, vmem_limit_bytes=48 * 1024 * 1024
        ),
        cost_estimate=pl.CostEstimate(flops=3_000_000_000, bytes_accessed=8_000_000, transcendentals=221_184),
    )(
        grid_field,
        disco_filter,
        offsets,
        disco_weight.reshape(KERNELS * C, C),
        jnp.swapaxes(legendre.reshape(MS, LMAX, LEG), 1, 2),
        spec_weight,
        degree_gain,
        *constant_tables(),
    )


def solution(mesh):
    in_specs = (
        P("lat", "lon", None),
        P(None, None, "lat"),
        P(None, None, "lat"),
        P(),
        P(None, "lat", None, "lon"),
        P(),
        P(),
    )
    out_specs = P("lat", "lon", None)
    return jax.shard_map(
        on_device, mesh=mesh, in_specs=in_specs, out_specs=out_specs, check_vma=False
    )
```

```python
import math

import jax
import jax.numpy as jnp
import numpy as np
from jax import lax
from jax.experimental import pallas as pl
from jax.experimental.pallas import tpu as pltpu
from jax.sharding import PartitionSpec as P

C = 384
NLAT = 384
NLON = 768
MMAX = 384
LMAX = 384
KERNELS = 3
LAT = 32
LON = 16
BAND = NLAT // LAT
TILE = NLON // LON
MS = 12
LEG = NLAT // LON
CHUNKS = 3
CW = C // CHUNKS
MESH = pl.DeviceIdType.MESH


def constant_tables():
    group = np.arange(LAT)[:, None, None, None]
    half = np.arange(2)[None, :, None, None]
    pair = np.arange(6)[None, None, :, None]
    index = group * 6 + pair
    wavenumber = np.where(half == 0, index, MMAX - 1 - index) + np.zeros((1, 1, 1, 2), np.int64)
    component = np.zeros_like(wavenumber) + np.arange(2)
    wavenumber = wavenumber.reshape(-1)
    component = component.reshape(-1)
    phases = (wavenumber[:, None] * np.arange(NLON)[None, :]) % NLON
    angles = phases.astype(np.float32) * np.float32(2.0 * math.pi / NLON)
    values = np.where(component[:, None] == 0, np.cos(angles), -np.sin(angles))
    values = values.astype(np.float32) * np.float32(1.0 / math.sqrt(NLON))
    table = jnp.asarray(values, jnp.bfloat16)
    table_t = jnp.asarray(values.T.copy(), jnp.bfloat16)
    perm = np.zeros((2 * MMAX, 2 * MMAX), np.float32)
    for band in range(LAT):
        for inner in range(2 * MS):
            perm[inner * LAT + band, band * 2 * MS + inner] = 1.0
    perm_leg = np.zeros((NLAT, NLAT), np.float32)
    for t in range(NLAT):
        perm_leg[(t % BAND) * LAT + t // BAND, t] = 1.0
    return (
        table,
        table_t,
        jnp.asarray(perm, jnp.bfloat16),
        jnp.asarray(perm.T.copy(), jnp.bfloat16),
        jnp.asarray(perm_leg, jnp.bfloat16),
    )


def dot(a, b):
    return jnp.dot(a, b, preferred_element_type=jnp.float32)


def kernel(
    grid_hbm, filt, offs, dw_hbm, leg_hbm, sw_hbm, gain_hbm, tab_hbm, tabt_hbm, pf_hbm, pb_hbm, pl_hbm,
    out_ref,
    grid_v, pad, dw, sw, gain, tab, tabt, pf, pb, pleg,
    legrecv, legp, legn, rows, fsend, frecv, gsend, hrecv, spec, rsend, gback, bsend, ret, ssend, srecv,
    basis, disco,
    load_sem, x1_send, x1_recv, leg_send, leg_recv, halo_send, halo_recv,
    a_send, a_recv, b_send, b_recv, c_send, c_recv, d_send, d_recv, e_send, e_recv,
):
    bf16 = jnp.bfloat16
    f32 = jnp.float32
    lat = lax.axis_index("lat")
    lon = lax.axis_index("lon")
    y = lax.div(lon, 2)
    z = lax.div(lat, 4)
    x = lax.rem(lat, 4)

    def has_row(device, ch):
        return lax.rem(device, 4) != ch

    def row_of(device, ch):
        inner = lax.rem(device, 4)
        return 3 * lax.div(device, 4) + jnp.where(inner > ch, inner - 1, inner)

    def has_wavenumber(device):
        inner = lax.rem(device, 8)
        return jnp.logical_and(inner != 5, inner != 7)

    def wavenumber_of(device):
        return 6 * lax.div(device, 8) + jnp.minimum(lax.rem(device, 8), 5)

    def ring(step):
        near = 4 - lax.div(step + 1, 2)
        return lax.rem(jnp.where(lax.rem(step, 2) == 0, 8 - near, near), 8)

    my_wavenumber = wavenumber_of(lon)

    north = lax.rem(lat + LAT - 1, LAT)
    south = lax.rem(lat + 1, LAT)
    west = lax.rem(lon + LON - 1, LON)
    east = lax.rem(lon + 1, LON)

    loads = [
        pltpu.make_async_copy(src, dst, load_sem.at[n])
        for n, (src, dst) in enumerate(
            (
                (grid_hbm, grid_v), (tab_hbm, tab), (pf_hbm, pf), (pl_hbm, pleg),
                (dw_hbm, dw), (sw_hbm, sw), (gain_hbm, gain), (pb_hbm, pb), (tabt_hbm, tabt),
            )
        )
    ]
    load_grid, load_tab, load_pf, load_pleg, load_dw, load_sw, load_gain, load_pb, load_tabt = loads
    for load in loads:
        load.start()

    barrier = pltpu.get_barrier_semaphore()

    def greet(device):
        pl.semaphore_signal(barrier, inc=1, device_id=device, device_id_type=MESH)

    @pl.loop(1, LON)
    def _(d):
        greet((lat, lax.rem(lon + d, LON)))

    @pl.loop(1, LAT)
    def _(d):
        greet((lax.rem(lat + d, LAT), lon))

    for a in (north, south):
        for b in (west, east):
            greet((a, b))
    pl.semaphore_wait(barrier, LON - 1 + LAT - 1 + 4)

    def remote(src, dst, send, recv, device):
        return pltpu.make_async_remote_copy(
            src_ref=src, dst_ref=dst, send_sem=send, recv_sem=recv, device_id=device, device_id_type=MESH
        )

    def along_lon(takes, number, source, target, send, recv):
        @pl.loop(0, LON)
        def _(step):
            there = 2 * lax.rem(y + ring(lax.div(step, 2)), 8) + lax.rem(step, 2)
            block = number(there)
            taken = takes(there)

            @pl.when(jnp.logical_and(taken, there != lon))
            def _():
                remote(source(block), target, send, recv, (lat, there)).start()

            @pl.when(jnp.logical_and(taken, there == lon))
            def _():
                pltpu.make_async_copy(source(block), target, recv).start()

    def to_rows(ch, source, target, send, recv):
        along_lon(lambda d: has_row(d, ch), lambda d: row_of(d, ch), source, target, send, recv)

    def to_wavenumbers(source, target, send, recv):
        along_lon(has_wavenumber, wavenumber_of, source, target, send, recv)

    def to_tiles(source, target, send, recv):
        along_lon(lambda d: d >= 0, lambda d: d, source, target, send, recv)

    def to_bands(source, target, send, recv):
        @pl.loop(0, LAT)
        def _(step):
            there = 4 * lax.rem(z + ring(lax.div(step, 4)), 8) + lax.rem(x + 2 + lax.rem(step, 4), 4)

            @pl.when(there != lat)
            def _():
                remote(source(there), target, send, recv, (there, lon)).start()

        pltpu.make_async_copy(source(lat), target, recv).start()

    def wait(ref, sem):
        pltpu.make_async_copy(ref, ref, sem).wait()

    for ch in range(CHUNKS):
        to_rows(
            ch, lambda row: grid_hbm.at[row, :, pl.ds(ch * CW, CW)], rows.at[ch, lon], x1_send.at[ch], x1_recv.at[ch]
        )

    load_grid.wait()
    for ct in range(C // 128):
        pad[ct, 2 : 2 + BAND, 8 : 8 + TILE, :] = grid_v[:, :, ct * 128 : (ct + 1) * 128].astype(f32)
    n0, n1 = 8, 8 + TILE
    t0, t1 = 2, 2 + BAND
    halo = [
        remote(
            pad.at[:, pl.ds(sr, nr), pl.ds(sc, nc), :], pad.at[:, pl.ds(dr, nr), pl.ds(dc, nc), :],
            halo_send.at[n], halo_recv.at[n], device,
        )
        for n, (sr, nr, sc, nc, dr, dc, device) in enumerate(
            (
                (t0, BAND, n0, 8, t0, n1, (lat, west)),
                (t0, BAND, n1 - 8, 8, t0, 0, (lat, east)),
                (t0, 2, n0, TILE, t1, n0, (north, lon)),
                (t1 - 2, 2, n0, TILE, 0, n0, (south, lon)),
                (t0, 2, n0, 8, t1, n1, (north, west)),
                (t0, 2, n1 - 8, 8, t1, 0, (north, east)),
                (t1 - 2, 2, n0, 8, 0, n1, (south, west)),
                (t1 - 2, 2, n1 - 8, 8, 0, 0, (south, east)),
            )
        )
    ]
    def send_halo():
        for copy in halo:
            copy.start()

    send_halo()

    def send_legendre():
        to_wavenumbers(lambda m: leg_hbm.at[m], legrecv.at[lon], leg_send, leg_recv)

    def forward_fourier(ch):
        wait(rows.at[ch], x1_recv.at[ch])

        part = dot(tab[...], rows[ch].reshape(NLON, CW))
        fsend[ch] = part.reshape(LAT, 2 * MS, CW).astype(bf16)

    def send_a(ch):
        to_bands(lambda q: fsend.at[ch, q], frecv.at[ch, lat], a_send.at[ch], a_recv.at[ch])

    def order_legendre():
        wait(legrecv, leg_recv)
        shards = legrecv[...].astype(f32).reshape(NLAT, LMAX).astype(bf16)
        ordered = dot(pleg[...], shards)
        legp[...] = ordered.astype(bf16)
        legn[...] = ordered.T.astype(bf16)

    def by_wavenumber(ch):
        wait(frecv.at[ch], a_recv.at[ch])
        got = frecv[ch].astype(f32).reshape(2 * MMAX, CW).astype(bf16)
        gsend[ch] = dot(pf[...], got).reshape(MS, 2 * LAT, CW).astype(bf16)

    def send_b(ch):
        to_wavenumbers(lambda m: gsend.at[ch, m], hrecv.at[ch, row_of(lon, ch)], b_send.at[ch], b_recv.at[ch])

    def stencil():
        @pl.loop(0, BAND)
        def _(i):
            for k in range(KERNELS):
                totals = [jnp.zeros((TILE, 128), f32)] * (C // 128)
                for j in range(5):
                    t = lat * BAND + i + (j - 2)
                    inside = jnp.logical_and(t >= 0, t < NLAT)
                    scale = jnp.where(inside, filt[j, k, i], 0.0)
                    first = 8 + offs[j, k, i]
                    totals = [
                        total + scale * pad[ct, i + j, pl.ds(first, TILE), :] for ct, total in enumerate(totals)
                    ]
                for ct, total in enumerate(totals):
                    at = k * C + ct * 128
                    basis[pl.ds(i * TILE, TILE), at : at + 128] = total.astype(bf16)

        @pl.loop(0, 4)
        def _(b):
            disco[pl.ds(b * 144, 144), :] = dot(basis[pl.ds(b * 144, 144), :], dw[...])

    def legendre(ch):
        wait(hrecv.at[ch], b_recv.at[ch])
        for r in range(2):
            part = hrecv[ch, :, r * LAT : (r + 1) * LAT, :].reshape(NLAT, CW)
            spec[:, r * C + ch * CW : r * C + (ch + 1) * CW] = dot(legn[...], part).astype(bf16)

    def mix_and_back(ch):
        cols = slice(ch * CW, (ch + 1) * CW)
        re = spec[:, :C]
        im = spec[:, C:]
        filtered = (
            dot(re, sw[0, :, cols]) - dot(im, sw[1, :, cols]),
            dot(re, sw[1, :, cols]) + dot(im, sw[0, :, cols]),
        )
        for r in range(2):
            value = (filtered[r] * gain[:, cols]).astype(bf16)
            back = dot(legp[...], value)
            rsend[ch, :, r * LAT : (r + 1) * LAT, :] = back.astype(bf16).reshape(BAND, LAT, CW)

    def send_c(ch):
        to_rows(ch, lambda row: rsend.at[ch, row], gback.at[ch, my_wavenumber], c_send.at[ch], c_recv.at[ch])

    def by_band(ch):
        wait(gback.at[ch], c_recv.at[ch])

        part = dot(pb[...], gback[ch].reshape(2 * MMAX, CW))
        bsend[ch] = part.reshape(LAT, 2 * MS, CW).astype(bf16)

    def send_d(ch):
        to_bands(lambda q: bsend.at[ch, q], ret.at[ch, lat], d_send.at[ch], d_recv.at[ch])

    def inverse_fourier(ch):
        wait(ret.at[ch], d_recv.at[ch])
        got = ret[ch].astype(f32).reshape(2 * MMAX, CW).astype(bf16)
        ssend[ch] = dot(tabt[...], got).reshape(LON, TILE, CW).astype(bf16)

    def send_e(ch):
        to_tiles(lambda n: ssend.at[ch, n], srecv.at[ch, row_of(lon, ch)], e_send.at[ch], e_recv.at[ch])

    def with_row(ch, step):
        @pl.when(has_row(lon, ch))
        def _():
            step(ch)

    def with_wavenumber(step):
        @pl.when(has_wavenumber(lon))
        def _():
            step()

    load_tab.wait()
    send_legendre()
    for ch in range(CHUNKS):
        with_row(ch, lambda ch: (forward_fourier(ch), send_a(ch)))
    load_pf.wait()
    for ch in range(CHUNKS):
        with_row(ch, lambda ch: (by_wavenumber(ch), send_b(ch)))

    load_pleg.wait()
    load_sw.wait()
    load_gain.wait()
    with_wavenumber(order_legendre)

    load_dw.wait()
    load_pb.wait()
    load_tabt.wait()
    for copy in halo:
        copy.wait_recv()
    stencil()

    @pl.when(has_wavenumber(lon))
    def _():
        for ch in range(CHUNKS):
            legendre(ch)
        for ch in range(CHUNKS):
            mix_and_back(ch)
            send_c(ch)

    for ch in range(CHUNKS):
        with_row(ch, lambda ch: (by_band(ch), send_d(ch)))
    for ch in range(CHUNKS):
        with_row(ch, lambda ch: (inverse_fourier(ch), send_e(ch)))

    for ch in range(CHUNKS):
        cols = slice(ch * CW, (ch + 1) * CW)
        wait(srecv.at[ch], e_recv.at[ch])

        @pl.loop(0, BAND)
        def _(i):
            combined = srecv[ch, i].astype(f32) + disco[pl.ds(i * TILE, TILE), cols]
            out_ref[i, :, cols] = (grid_v[i, :, cols].astype(f32) + jax.nn.gelu(combined)).astype(bf16)

    for copy in halo:
        copy.wait_send()
    for ch in range(CHUNKS):
        mine = has_row(lon, ch)

        @pl.when(mine)
        def _():
            wait(rows.at[ch, pl.ds(0, BAND - 1)], x1_send.at[ch])
            wait(fsend.at[ch, pl.ds(0, LAT - 1)], a_send.at[ch])
            wait(bsend.at[ch, pl.ds(0, LAT - 1)], d_send.at[ch])
            wait(ssend.at[ch, pl.ds(0, LON - 1)], e_send.at[ch])

        @pl.when(jnp.logical_not(mine))
        def _():
            wait(rows.at[ch, pl.ds(0, BAND)], x1_send.at[ch])

        @pl.when(jnp.logical_and(mine, has_wavenumber(lon)))
        def _():
            wait(gsend.at[ch, pl.ds(0, MS - 1)], b_send.at[ch])
            wait(rsend.at[ch, pl.ds(0, BAND - 1)], c_send.at[ch])

        @pl.when(jnp.logical_and(mine, jnp.logical_not(has_wavenumber(lon))))
        def _():
            wait(gsend.at[ch], b_send.at[ch])

        @pl.when(jnp.logical_and(jnp.logical_not(mine), has_wavenumber(lon)))
        def _():
            wait(rsend.at[ch], c_send.at[ch])

    @pl.when(has_wavenumber(lon))
    def _():
        wait(legrecv.at[pl.ds(0, MS - 1)], leg_send)

    @pl.when(jnp.logical_not(has_wavenumber(lon)))
    def _():
        wait(legrecv.at[pl.ds(0, MS)], leg_send)


def on_device(grid_field, disco_filter, offsets, disco_weight, legendre, spec_weight, degree_gain):
    bf16 = jnp.bfloat16
    f32 = jnp.float32
    smem = pl.BlockSpec(memory_space=pltpu.SMEM)
    hbm = pl.BlockSpec(memory_space=pltpu.HBM)
    dma = pltpu.SemaphoreType.DMA
    vmem = pltpu.VMEM
    return pl.pallas_call(
        kernel,
        out_shape=jax.ShapeDtypeStruct(grid_field.shape, bf16),
        in_specs=[hbm, smem, smem] + [hbm] * 9,
        out_specs=pl.BlockSpec(memory_space=pltpu.VMEM),
        scratch_shapes=[
            vmem((BAND, TILE, C), bf16),
            vmem((C // 128, BAND + 4, TILE + 16, 128), f32),
            vmem((KERNELS * C, C), bf16),
            vmem((2, C, C), bf16),
            vmem((LMAX, C), f32),
            vmem((2 * MMAX, NLON), bf16),
            vmem((NLON, 2 * MMAX), bf16),
            vmem((2 * MMAX, 2 * MMAX), bf16),
            vmem((2 * MMAX, 2 * MMAX), bf16),
            vmem((NLAT, NLAT), bf16),
            vmem((LON, LEG, LMAX), bf16),
            vmem((NLAT, LMAX), bf16),
            vmem((LMAX, NLAT), bf16),
            vmem((CHUNKS, LON, TILE, CW), bf16),
            vmem((CHUNKS, LAT, 2 * MS, CW), bf16),
            vmem((CHUNKS, LAT, 2 * MS, CW), bf16),
            vmem((CHUNKS, MS, 2 * LAT, CW), bf16),
            vmem((CHUNKS, BAND, 2 * LAT, CW), bf16),
            vmem((LMAX, 2 * C), bf16),
            vmem((CHUNKS, BAND, 2 * LAT, CW), bf16),
            vmem((CHUNKS, MS, 2 * LAT, CW), bf16),
            vmem((CHUNKS, LAT, 2 * MS, CW), bf16),
            vmem((CHUNKS, LAT, 2 * MS, CW), bf16),
            vmem((CHUNKS, LON, TILE, CW), bf16),
            vmem((CHUNKS, BAND, TILE, CW), bf16),
            vmem((BAND * TILE, KERNELS * C), bf16),
            vmem((BAND * TILE, C), f32),
            dma((9,)),
            dma((CHUNKS,)), dma((CHUNKS,)),
            dma, dma,
            dma((8,)), dma((8,)),
            dma((CHUNKS,)), dma((CHUNKS,)),
            dma((CHUNKS,)), dma((CHUNKS,)),
            dma((CHUNKS,)), dma((CHUNKS,)),
            dma((CHUNKS,)), dma((CHUNKS,)),
            dma((CHUNKS,)), dma((CHUNKS,)),
        ],
        compiler_params=pltpu.CompilerParams(
            collective_id=0, has_side_effects=True, vmem_limit_bytes=62 * 1024 * 1024
        ),
        cost_estimate=pl.CostEstimate(flops=3_000_000_000, bytes_accessed=8_000_000, transcendentals=221_184),
    )(
        grid_field,
        jnp.swapaxes(disco_filter, 0, 1),
        jnp.swapaxes(offsets, 0, 1),
        disco_weight.reshape(KERNELS * C, C),
        jnp.swapaxes(legendre.reshape(MS, LMAX, LEG), 1, 2),
        spec_weight,
        degree_gain,
        *constant_tables(),
    )


def solution(mesh):
    in_specs = (
        P("lat", "lon", None),
        P(None, None, "lat"),
        P(None, None, "lat"),
        P(),
        P(None, "lat", None, "lon"),
        P(),
        P(),
    )
    out_specs = P("lat", "lon", None)
    return jax.shard_map(
        on_device, mesh=mesh, in_specs=in_specs, out_specs=out_specs, check_vma=False
    )
```

```python
import math

import jax
import jax.numpy as jnp
import numpy as np
from jax import lax
from jax.experimental import pallas as pl
from jax.experimental.pallas import tpu as pltpu
from jax.sharding import PartitionSpec as P

C = 384
NLAT = 384
NLON = 768
MMAX = 384
LMAX = 384
KERNELS = 3
LAT = 32
LON = 16
BAND = NLAT // LAT
TILE = NLON // LON
MS = 12
LEG = NLAT // LON
CHUNKS = 3
CW = C // CHUNKS
MESH = pl.DeviceIdType.MESH


def constant_tables():
    group = np.arange(LAT)[:, None, None, None]
    half = np.arange(2)[None, :, None, None]
    pair = np.arange(6)[None, None, :, None]
    index = group * 6 + pair
    wavenumber = np.where(half == 0, index, MMAX - 1 - index) + np.zeros((1, 1, 1, 2), np.int64)
    component = np.zeros_like(wavenumber) + np.arange(2)
    wavenumber = wavenumber.reshape(-1)
    component = component.reshape(-1)
    phases = (wavenumber[:, None] * np.arange(NLON)[None, :]) % NLON
    angles = phases.astype(np.float32) * np.float32(2.0 * math.pi / NLON)
    values = np.where(component[:, None] == 0, np.cos(angles), -np.sin(angles))
    values = values.astype(np.float32) * np.float32(1.0 / math.sqrt(NLON))
    table = jnp.asarray(values, jnp.bfloat16)
    table_t = jnp.asarray(values.T.copy(), jnp.bfloat16)
    perm = np.zeros((2 * MMAX, 2 * MMAX), np.float32)
    for band in range(LAT):
        for inner in range(2 * MS):
            perm[inner * LAT + band, band * 2 * MS + inner] = 1.0
    perm_leg = np.zeros((NLAT, NLAT), np.float32)
    for t in range(NLAT):
        perm_leg[(t % BAND) * LAT + t // BAND, t] = 1.0
    return (
        table,
        table_t,
        jnp.asarray(perm, jnp.bfloat16),
        jnp.asarray(perm.T.copy(), jnp.bfloat16),
        jnp.asarray(perm_leg, jnp.bfloat16),
    )


def dot(a, b):
    return jnp.dot(a, b, preferred_element_type=jnp.float32)


def kernel(
    grid_hbm, filt_hbm, offs_hbm, dw_hbm, leg_hbm, sw_hbm, gain_hbm, tab_hbm, tabt_hbm, pf_hbm, pb_hbm, pl_hbm,
    tiles, disco,
    grid_v, pad, dw, sw, gain, tab, tabt, pf, pb, pleg,
    filt, offs, legrecv, legp, legn, rows, fsend, frecv, gsend, hrecv, spec, rsend, gback, bsend, ret, ssend,
    basis,
    load_sem, x1_send, x1_recv, leg_send, leg_recv, halo_send, halo_recv,
    a_send, a_recv, b_send, b_recv, c_send, c_recv, d_send, d_recv, e_send, e_recv,
):
    bf16 = jnp.bfloat16
    f32 = jnp.float32
    lat = lax.axis_index("lat")
    lon = lax.axis_index("lon")
    y = lax.div(lon, 2)
    z = lax.div(lat, 4)
    x = lax.rem(lat, 4)

    def has_row(device, ch):
        return lax.rem(device, 4) != ch

    def row_of(device, ch):
        inner = lax.rem(device, 4)
        return 3 * lax.div(device, 4) + jnp.where(inner > ch, inner - 1, inner)

    def has_wavenumber(device):
        inner = lax.rem(device, 8)
        return jnp.logical_and(inner != 5, inner != 7)

    def wavenumber_of(device):
        return 6 * lax.div(device, 8) + jnp.minimum(lax.rem(device, 8), 5)

    def ring(step):
        near = 4 - lax.div(step + 1, 2)
        return lax.rem(jnp.where(lax.rem(step, 2) == 0, 8 - near, near), 8)

    my_wavenumber = wavenumber_of(lon)

    north = lax.rem(lat + LAT - 1, LAT)
    south = lax.rem(lat + 1, LAT)
    west = lax.rem(lon + LON - 1, LON)
    east = lax.rem(lon + 1, LON)

    loads = [
        pltpu.make_async_copy(src, dst, load_sem.at[n])
        for n, (src, dst) in enumerate(
            (
                (grid_hbm, grid_v), (tab_hbm, tab), (pf_hbm, pf), (pl_hbm, pleg),
                (dw_hbm, dw), (sw_hbm, sw), (gain_hbm, gain), (pb_hbm, pb), (tabt_hbm, tabt), (filt_hbm, filt), (offs_hbm, offs),
            )
        )
    ]
    load_grid, load_tab, load_pf, load_pleg, load_dw, load_sw, load_gain, load_pb, load_tabt, load_filt, load_offs = loads
    barrier = pltpu.get_barrier_semaphore()

    def greet(device):
        pl.semaphore_signal(barrier, inc=1, device_id=device, device_id_type=MESH)

    @pl.loop(1, LON)
    def _(d):
        greet((lat, lax.rem(lon + d, LON)))

    @pl.loop(1, LAT)
    def _(d):
        greet((lax.rem(lat + d, LAT), lon))

    for a in (north, south):
        for b in (west, east):
            greet((a, b))
    pl.semaphore_wait(barrier, LON - 1 + LAT - 1 + 4)

    def remote(src, dst, send, recv, device):
        return pltpu.make_async_remote_copy(
            src_ref=src, dst_ref=dst, send_sem=send, recv_sem=recv, device_id=device, device_id_type=MESH
        )

    def along_lon(takes, number, source, target, send, recv):
        @pl.loop(0, LON)
        def _(step):
            there = 2 * lax.rem(y + ring(lax.div(step, 2)), 8) + lax.rem(step, 2)
            block = number(there)
            taken = takes(there)

            @pl.when(jnp.logical_and(taken, there != lon))
            def _():
                remote(source(block), target, send, recv, (lat, there)).start()

            @pl.when(jnp.logical_and(taken, there == lon))
            def _():
                pltpu.make_async_copy(source(block), target, recv).start()

    def to_rows(ch, source, target, send, recv):
        along_lon(lambda d: has_row(d, ch), lambda d: row_of(d, ch), source, target, send, recv)

    def to_wavenumbers(source, target, send, recv):
        along_lon(has_wavenumber, wavenumber_of, source, target, send, recv)

    def to_tiles(source, target, send, recv):
        along_lon(lambda d: d >= 0, lambda d: d, source, target, send, recv)

    def to_bands(source, target, send, recv):
        @pl.loop(0, LAT)
        def _(step):
            there = 4 * lax.rem(z + ring(lax.div(step, 4)), 8) + lax.rem(x + 2 + lax.rem(step, 4), 4)

            @pl.when(there != lat)
            def _():
                remote(source(there), target, send, recv, (there, lon)).start()

        pltpu.make_async_copy(source(lat), target, recv).start()

    def wait(ref, sem):
        pltpu.make_async_copy(ref, ref, sem).wait()

    for ch in range(CHUNKS):
        to_rows(
            ch, lambda row: grid_hbm.at[row, :, pl.ds(ch * CW, CW)], rows.at[ch, lon], x1_send.at[ch], x1_recv.at[ch]
        )

    for load in loads:
        load.start()

    load_grid.wait()
    for ct in range(C // 128):
        pad[ct, 2 : 2 + BAND, 8 : 8 + TILE, :] = grid_v[:, :, ct * 128 : (ct + 1) * 128].astype(f32)
    n0, n1 = 8, 8 + TILE
    t0, t1 = 2, 2 + BAND
    halo = [
        remote(
            pad.at[:, pl.ds(sr, nr), pl.ds(sc, nc), :], pad.at[:, pl.ds(dr, nr), pl.ds(dc, nc), :],
            halo_send.at[n], halo_recv.at[n], device,
        )
        for n, (sr, nr, sc, nc, dr, dc, device) in enumerate(
            (
                (t0, BAND, n0, 8, t0, n1, (lat, west)),
                (t0, BAND, n1 - 8, 8, t0, 0, (lat, east)),
                (t0, 2, n0, TILE, t1, n0, (north, lon)),
                (t1 - 2, 2, n0, TILE, 0, n0, (south, lon)),
                (t0, 2, n0, 8, t1, n1, (north, west)),
                (t0, 2, n1 - 8, 8, t1, 0, (north, east)),
                (t1 - 2, 2, n0, 8, 0, n1, (south, west)),
                (t1 - 2, 2, n1 - 8, 8, 0, 0, (south, east)),
            )
        )
    ]
    def send_halo():
        for copy in halo:
            copy.start()

    send_halo()

    def send_legendre():
        to_wavenumbers(lambda m: leg_hbm.at[m], legrecv.at[lon], leg_send, leg_recv)

    def forward_fourier(ch):
        wait(rows.at[ch], x1_recv.at[ch])

        part = dot(tab[...], rows[ch].reshape(NLON, CW))
        fsend[ch] = part.reshape(LAT, 2 * MS, CW).astype(bf16)

    def send_a(ch):
        to_bands(lambda q: fsend.at[ch, q], frecv.at[ch, lat], a_send.at[ch], a_recv.at[ch])

    def order_legendre():
        wait(legrecv, leg_recv)
        shards = legrecv[...].astype(f32).reshape(NLAT, LMAX).astype(bf16)
        ordered = dot(pleg[...], shards)
        legp[...] = ordered.astype(bf16)
        legn[...] = ordered.T.astype(bf16)

    def by_wavenumber(ch):
        wait(frecv.at[ch], a_recv.at[ch])
        got = frecv[ch].astype(f32).reshape(2 * MMAX, CW).astype(bf16)
        gsend[ch] = dot(pf[...], got).reshape(MS, 2 * LAT, CW).astype(bf16)

    def send_b(ch):
        to_wavenumbers(lambda m: gsend.at[ch, m], hrecv.at[ch, row_of(lon, ch)], b_send.at[ch], b_recv.at[ch])

    def stencil():
        @pl.loop(0, BAND)
        def _(i):
            for k in range(KERNELS):
                totals = [jnp.zeros((TILE, 128), f32)] * (C // 128)
                for j in range(5):
                    t = lat * BAND + i + (j - 2)
                    inside = jnp.logical_and(t >= 0, t < NLAT)
                    scale = jnp.where(inside, filt[j, k, i], 0.0)
                    first = 8 + offs[j, k, i]
                    totals = [
                        total + scale * pad[ct, i + j, pl.ds(first, TILE), :] for ct, total in enumerate(totals)
                    ]
                for ct, total in enumerate(totals):
                    at = k * C + ct * 128
                    basis[pl.ds(i * TILE, TILE), at : at + 128] = total.astype(bf16)

        @pl.loop(0, 4)
        def _(b):
            disco[pl.ds(b * 144, 144), :] = dot(basis[pl.ds(b * 144, 144), :], dw[...])

    def legendre(ch):
        wait(hrecv.at[ch], b_recv.at[ch])
        for r in range(2):
            part = hrecv[ch, :, r * LAT : (r + 1) * LAT, :].reshape(NLAT, CW)
            spec[:, r * C + ch * CW : r * C + (ch + 1) * CW] = dot(legn[...], part).astype(bf16)

    def mix_and_back(ch):
        cols = slice(ch * CW, (ch + 1) * CW)
        re = spec[:, :C]
        im = spec[:, C:]
        filtered = (
            dot(re, sw[0, :, cols]) - dot(im, sw[1, :, cols]),
            dot(re, sw[1, :, cols]) + dot(im, sw[0, :, cols]),
        )
        for r in range(2):
            value = (filtered[r] * gain[:, cols]).astype(bf16)
            back = dot(legp[...], value)
            rsend[ch, :, r * LAT : (r + 1) * LAT, :] = back.astype(bf16).reshape(BAND, LAT, CW)

    def send_c(ch):
        to_rows(ch, lambda row: rsend.at[ch, row], gback.at[ch, my_wavenumber], c_send.at[ch], c_recv.at[ch])

    def by_band(ch):
        wait(gback.at[ch], c_recv.at[ch])

        part = dot(pb[...], gback[ch].reshape(2 * MMAX, CW))
        bsend[ch] = part.reshape(LAT, 2 * MS, CW).astype(bf16)

    def send_d(ch):
        to_bands(lambda q: bsend.at[ch, q], ret.at[ch, lat], d_send.at[ch], d_recv.at[ch])

    def inverse_fourier(ch):
        wait(ret.at[ch], d_recv.at[ch])
        got = ret[ch].astype(f32).reshape(2 * MMAX, CW).astype(bf16)
        ssend[ch] = dot(tabt[...], got).reshape(LON, TILE, CW).astype(bf16)

    def send_e(ch):
        here = tiles.at[row_of(lon, ch), :, pl.ds(ch * CW, CW)]
        to_tiles(lambda n: ssend.at[ch, n], here, e_send.at[ch], e_recv)

    def with_row(ch, step):
        @pl.when(has_row(lon, ch))
        def _():
            step(ch)

    def with_wavenumber(step):
        @pl.when(has_wavenumber(lon))
        def _():
            step()

    load_tab.wait()
    send_legendre()
    for ch in range(CHUNKS):
        with_row(ch, lambda ch: (forward_fourier(ch), send_a(ch)))
    load_pf.wait()
    for ch in range(CHUNKS):
        with_row(ch, lambda ch: (by_wavenumber(ch), send_b(ch)))

    load_pleg.wait()
    load_sw.wait()
    load_gain.wait()
    with_wavenumber(order_legendre)

    load_dw.wait()
    load_filt.wait()
    load_offs.wait()
    load_pb.wait()
    load_tabt.wait()
    for copy in halo:
        copy.wait_recv()
    stencil()

    @pl.when(has_wavenumber(lon))
    def _():
        for ch in range(CHUNKS):
            legendre(ch)
        for ch in range(CHUNKS):
            mix_and_back(ch)
            send_c(ch)

    for ch in range(CHUNKS):
        with_row(ch, lambda ch: (by_band(ch), send_d(ch)))
    for ch in range(CHUNKS):
        with_row(ch, lambda ch: (inverse_fourier(ch), send_e(ch)))

    wait(tiles, e_recv)

    for copy in halo:
        copy.wait_send()
    for ch in range(CHUNKS):
        mine = has_row(lon, ch)

        @pl.when(mine)
        def _():
            wait(rows.at[ch, pl.ds(0, BAND - 1)], x1_send.at[ch])
            wait(fsend.at[ch, pl.ds(0, LAT - 1)], a_send.at[ch])
            wait(bsend.at[ch, pl.ds(0, LAT - 1)], d_send.at[ch])
            wait(ssend.at[ch, pl.ds(0, LON - 1)], e_send.at[ch])

        @pl.when(jnp.logical_not(mine))
        def _():
            wait(rows.at[ch, pl.ds(0, BAND)], x1_send.at[ch])

        @pl.when(jnp.logical_and(mine, has_wavenumber(lon)))
        def _():
            wait(gsend.at[ch, pl.ds(0, MS - 1)], b_send.at[ch])
            wait(rsend.at[ch, pl.ds(0, BAND - 1)], c_send.at[ch])

        @pl.when(jnp.logical_and(mine, jnp.logical_not(has_wavenumber(lon))))
        def _():
            wait(gsend.at[ch], b_send.at[ch])

        @pl.when(jnp.logical_and(jnp.logical_not(mine), has_wavenumber(lon)))
        def _():
            wait(rsend.at[ch], c_send.at[ch])

    @pl.when(has_wavenumber(lon))
    def _():
        wait(legrecv.at[pl.ds(0, MS - 1)], leg_send)

    @pl.when(jnp.logical_not(has_wavenumber(lon)))
    def _():
        wait(legrecv.at[pl.ds(0, MS)], leg_send)


def on_device(grid_field, disco_filter, offsets, disco_weight, legendre, spec_weight, degree_gain):
    bf16 = jnp.bfloat16
    f32 = jnp.float32
    hbm = pl.BlockSpec(memory_space=pltpu.HBM)
    dma = pltpu.SemaphoreType.DMA
    vmem = pltpu.VMEM
    spectral, disco = pl.pallas_call(
        kernel,
        out_shape=(
            vmem(grid_field.shape, bf16),
            vmem((BAND * TILE, C), f32),
        ),
        in_specs=[hbm] * 12,
        out_specs=(pl.BlockSpec(memory_space=pltpu.VMEM),) * 2,
        scratch_shapes=[
            vmem((BAND, TILE, C), bf16),
            vmem((C // 128, BAND + 4, TILE + 16, 128), f32),
            vmem((KERNELS * C, C), bf16),
            vmem((2, C, C), bf16),
            vmem((LMAX, C), f32),
            vmem((2 * MMAX, NLON), bf16),
            vmem((NLON, 2 * MMAX), bf16),
            vmem((2 * MMAX, 2 * MMAX), bf16),
            vmem((2 * MMAX, 2 * MMAX), bf16),
            vmem((NLAT, NLAT), bf16),
            pltpu.SMEM((5, KERNELS, BAND), f32),
            pltpu.SMEM((5, KERNELS, BAND), jnp.int32),
            vmem((LON, LEG, LMAX), bf16),
            vmem((NLAT, LMAX), bf16),
            vmem((LMAX, NLAT), bf16),
            vmem((CHUNKS, LON, TILE, CW), bf16),
            vmem((CHUNKS, LAT, 2 * MS, CW), bf16),
            vmem((CHUNKS, LAT, 2 * MS, CW), bf16),
            vmem((CHUNKS, MS, 2 * LAT, CW), bf16),
            vmem((CHUNKS, BAND, 2 * LAT, CW), bf16),
            vmem((LMAX, 2 * C), bf16),
            vmem((CHUNKS, BAND, 2 * LAT, CW), bf16),
            vmem((CHUNKS, MS, 2 * LAT, CW), bf16),
            vmem((CHUNKS, LAT, 2 * MS, CW), bf16),
            vmem((CHUNKS, LAT, 2 * MS, CW), bf16),
            vmem((CHUNKS, LON, TILE, CW), bf16),
            vmem((BAND * TILE, KERNELS * C), bf16),
            dma((11,)),
            dma((CHUNKS,)), dma((CHUNKS,)),
            dma, dma,
            dma((8,)), dma((8,)),
            dma((CHUNKS,)), dma((CHUNKS,)),
            dma((CHUNKS,)), dma((CHUNKS,)),
            dma((CHUNKS,)), dma((CHUNKS,)),
            dma((CHUNKS,)), dma((CHUNKS,)),
            dma((CHUNKS,)), dma,
        ],
        compiler_params=pltpu.CompilerParams(
            collective_id=0, has_side_effects=True, vmem_limit_bytes=62 * 1024 * 1024
        ),
        cost_estimate=pl.CostEstimate(flops=3_000_000_000, bytes_accessed=8_000_000, transcendentals=221_184),
    )(
        grid_field,
        jnp.swapaxes(disco_filter, 0, 1),
        jnp.swapaxes(offsets, 0, 1),
        disco_weight.reshape(KERNELS * C, C),
        jnp.swapaxes(legendre.reshape(MS, LMAX, LEG), 1, 2),
        spec_weight,
        degree_gain,
        *constant_tables(),
    )
    combined = spectral.astype(f32) + disco.reshape(grid_field.shape)
    return (grid_field.astype(f32) + jax.nn.gelu(combined)).astype(bf16)


def solution(mesh):
    in_specs = (
        P("lat", "lon", None),
        P(None, None, "lat"),
        P(None, None, "lat"),
        P(),
        P(None, "lat", None, "lon"),
        P(),
        P(),
    )
    out_specs = P("lat", "lon", None)
    return jax.shard_map(
        on_device, mesh=mesh, in_specs=in_specs, out_specs=out_specs, check_vma=False
    )
```

```python
import math

import jax
import jax.numpy as jnp
import numpy as np
from jax import lax
from jax.experimental import pallas as pl
from jax.experimental.pallas import tpu as pltpu
from jax.sharding import PartitionSpec as P

C = 384
NLAT = 384
NLON = 768
MMAX = 384
LMAX = 384
KERNELS = 3
LAT = 32
LON = 16
BAND = NLAT // LAT
TILE = NLON // LON
MS = 12
LEG = NLAT // LON
CHUNKS = 3
CW = C // CHUNKS
MESH = pl.DeviceIdType.MESH


def constant_tables():
    group = np.arange(LAT)[:, None, None, None]
    half = np.arange(2)[None, :, None, None]
    pair = np.arange(6)[None, None, :, None]
    index = group * 6 + pair
    wavenumber = np.where(half == 0, index, MMAX - 1 - index) + np.zeros((1, 1, 1, 2), np.int64)
    component = np.zeros_like(wavenumber) + np.arange(2)
    wavenumber = wavenumber.reshape(-1)
    component = component.reshape(-1)
    phases = (wavenumber[:, None] * np.arange(NLON)[None, :]) % NLON
    angles = phases.astype(np.float32) * np.float32(2.0 * math.pi / NLON)
    values = np.where(component[:, None] == 0, np.cos(angles), -np.sin(angles))
    values = values.astype(np.float32) * np.float32(1.0 / math.sqrt(NLON))
    table = jnp.asarray(values, jnp.bfloat16)
    table_t = jnp.asarray(values.T.copy(), jnp.bfloat16)
    perm_leg = np.zeros((NLAT, NLAT), np.float32)
    for t in range(NLAT):
        perm_leg[(t % BAND) * LAT + t // BAND, t] = 1.0
    return (
        table,
        table_t,
        jnp.asarray(perm_leg, jnp.bfloat16),
    )


def dot(a, b):
    return jnp.dot(a, b, preferred_element_type=jnp.float32)


def kernel(
    grid_hbm, filt_hbm, offs_hbm, dw_hbm, leg_hbm, sw_hbm, gain_hbm, tab_hbm, tabt_hbm, pl_hbm,
    tiles, disco,
    grid_v, pad, dw, sw, gain, tab, tabt, pleg,
    filt, offs, legrecv, legp, legn, rows, fsend, frecv, gsend, hrecv, spec, rsend, gback, bsend, ret, ssend,
    basis,
    load_sem, x1_send, x1_recv, leg_send, leg_recv, halo_send, halo_recv,
    a_send, a_recv, b_send, b_recv, c_send, c_recv, d_send, d_recv, e_send, e_recv,
):
    bf16 = jnp.bfloat16
    f32 = jnp.float32
    lat = lax.axis_index("lat")
    lon = lax.axis_index("lon")
    y = lax.div(lon, 2)
    z = lax.div(lat, 4)
    x = lax.rem(lat, 4)

    def has_row(device, ch):
        return lax.rem(device, 4) != ch

    def row_of(device, ch):
        inner = lax.rem(device, 4)
        return 3 * lax.div(device, 4) + jnp.where(inner > ch, inner - 1, inner)

    def has_wavenumber(device):
        inner = lax.rem(device, 8)
        return jnp.logical_and(inner != 5, inner != 7)

    def wavenumber_of(device):
        return 6 * lax.div(device, 8) + jnp.minimum(lax.rem(device, 8), 5)

    def ring(step):
        near = 4 - lax.div(step + 1, 2)
        return lax.rem(jnp.where(lax.rem(step, 2) == 0, 8 - near, near), 8)

    my_wavenumber = wavenumber_of(lon)

    north = lax.rem(lat + LAT - 1, LAT)
    south = lax.rem(lat + 1, LAT)
    west = lax.rem(lon + LON - 1, LON)
    east = lax.rem(lon + 1, LON)

    loads = [
        pltpu.make_async_copy(src, dst, load_sem.at[n])
        for n, (src, dst) in enumerate(
            (
                (grid_hbm, grid_v), (tab_hbm, tab), (pl_hbm, pleg),
                (dw_hbm, dw), (sw_hbm, sw), (gain_hbm, gain), (tabt_hbm, tabt), (filt_hbm, filt), (offs_hbm, offs),
            )
        )
    ]
    load_grid, load_tab, load_pleg, load_dw, load_sw, load_gain, load_tabt, load_filt, load_offs = loads
    barrier = pltpu.get_barrier_semaphore()

    def greet(device):
        pl.semaphore_signal(barrier, inc=1, device_id=device, device_id_type=MESH)

    @pl.loop(1, LON)
    def _(d):
        greet((lat, lax.rem(lon + d, LON)))

    @pl.loop(1, LAT)
    def _(d):
        greet((lax.rem(lat + d, LAT), lon))

    for a in (north, south):
        for b in (west, east):
            greet((a, b))
    pl.semaphore_wait(barrier, LON - 1 + LAT - 1 + 4)

    def remote(src, dst, send, recv, device):
        return pltpu.make_async_remote_copy(
            src_ref=src, dst_ref=dst, send_sem=send, recv_sem=recv, device_id=device, device_id_type=MESH
        )

    def along_lon(takes, number, source, target, send, recv):
        @pl.loop(0, LON)
        def _(step):
            there = 2 * lax.rem(y + ring(lax.div(step, 2)), 8) + lax.rem(step, 2)
            block = number(there)
            taken = takes(there)

            @pl.when(jnp.logical_and(taken, there != lon))
            def _():
                remote(source(block), target, send, recv, (lat, there)).start()

            @pl.when(jnp.logical_and(taken, there == lon))
            def _():
                pltpu.make_async_copy(source(block), target, recv).start()

    def to_rows(ch, source, target, send, recv):
        along_lon(lambda d: has_row(d, ch), lambda d: row_of(d, ch), source, target, send, recv)

    def to_wavenumbers(source, target, send, recv):
        along_lon(has_wavenumber, wavenumber_of, source, target, send, recv)

    def to_tiles(source, target, send, recv):
        along_lon(lambda d: d >= 0, lambda d: d, source, target, send, recv)

    def to_bands(source, target, send, recv):
        @pl.loop(0, LAT)
        def _(step):
            there = 4 * lax.rem(z + ring(lax.div(step, 4)), 8) + lax.rem(x + 2 + lax.rem(step, 4), 4)

            @pl.when(there != lat)
            def _():
                remote(source(there), target, send, recv, (there, lon)).start()

        pltpu.make_async_copy(source(lat), target, recv).start()

    def wait(ref, sem):
        pltpu.make_async_copy(ref, ref, sem).wait()

    for ch in range(CHUNKS):
        to_rows(
            ch, lambda row: grid_hbm.at[row, :, pl.ds(ch * CW, CW)], rows.at[ch, lon], x1_send.at[ch], x1_recv.at[ch]
        )

    for load in loads:
        load.start()

    load_grid.wait()
    for ct in range(C // 128):
        pad[ct, 2 : 2 + BAND, 8 : 8 + TILE, :] = grid_v[:, :, ct * 128 : (ct + 1) * 128].astype(f32)
    n0, n1 = 8, 8 + TILE
    t0, t1 = 2, 2 + BAND
    halo = [
        remote(
            pad.at[:, pl.ds(sr, nr), pl.ds(sc, nc), :], pad.at[:, pl.ds(dr, nr), pl.ds(dc, nc), :],
            halo_send.at[n], halo_recv.at[n], device,
        )
        for n, (sr, nr, sc, nc, dr, dc, device) in enumerate(
            (
                (t0, BAND, n0, 8, t0, n1, (lat, west)),
                (t0, BAND, n1 - 8, 8, t0, 0, (lat, east)),
                (t0, 2, n0, TILE, t1, n0, (north, lon)),
                (t1 - 2, 2, n0, TILE, 0, n0, (south, lon)),
                (t0, 2, n0, 8, t1, n1, (north, west)),
                (t0, 2, n1 - 8, 8, t1, 0, (north, east)),
                (t1 - 2, 2, n0, 8, 0, n1, (south, west)),
                (t1 - 2, 2, n1 - 8, 8, 0, 0, (south, east)),
            )
        )
    ]
    def send_halo():
        for copy in halo:
            copy.start()

    send_halo()

    def send_legendre():
        to_wavenumbers(lambda m: leg_hbm.at[m], legrecv.at[lon], leg_send, leg_recv)

    def forward_fourier(ch):
        wait(rows.at[ch], x1_recv.at[ch])

        part = dot(tab[...], rows[ch].reshape(NLON, CW))
        fsend[ch] = part.reshape(LAT, 2 * MS, CW).astype(bf16)

    def send_a(ch):
        to_bands(lambda q: fsend.at[ch, q], frecv.at[ch, lat], a_send.at[ch], a_recv.at[ch])

    def order_legendre():
        wait(legrecv, leg_recv)
        shards = legrecv[...].astype(f32).reshape(NLAT, LMAX).astype(bf16)
        ordered = dot(pleg[...], shards)
        legp[...] = ordered.astype(bf16)
        legn[...] = ordered.T.astype(bf16)

    def by_wavenumber(ch):
        wait(frecv.at[ch], a_recv.at[ch])
        turned = jnp.swapaxes(frecv[ch].astype(f32), 0, 1)
        gsend[ch] = turned.reshape(MS, 2 * LAT, CW).astype(bf16)

    def send_b(ch):
        to_wavenumbers(lambda m: gsend.at[ch, m], hrecv.at[ch, row_of(lon, ch)], b_send.at[ch], b_recv.at[ch])

    def stencil():
        @pl.loop(0, BAND)
        def _(i):
            for k in range(KERNELS):
                totals = [jnp.zeros((TILE, 128), f32)] * (C // 128)
                for j in range(5):
                    t = lat * BAND + i + (j - 2)
                    inside = jnp.logical_and(t >= 0, t < NLAT)
                    scale = jnp.where(inside, filt[j, k, i], 0.0)
                    first = 8 + offs[j, k, i]
                    totals = [
                        total + scale * pad[ct, i + j, pl.ds(first, TILE), :] for ct, total in enumerate(totals)
                    ]
                for ct, total in enumerate(totals):
                    at = k * C + ct * 128
                    basis[pl.ds(i * TILE, TILE), at : at + 128] = total.astype(bf16)

        @pl.loop(0, 4)
        def _(b):
            disco[pl.ds(b * 144, 144), :] = dot(basis[pl.ds(b * 144, 144), :], dw[...])

    def legendre(ch):
        wait(hrecv.at[ch], b_recv.at[ch])
        for r in range(2):
            part = hrecv[ch, :, r * LAT : (r + 1) * LAT, :].reshape(NLAT, CW)
            spec[:, r * C + ch * CW : r * C + (ch + 1) * CW] = dot(legn[...], part).astype(bf16)

    def mix_and_back(ch):
        cols = slice(ch * CW, (ch + 1) * CW)
        re = spec[:, :C]
        im = spec[:, C:]
        filtered = (
            dot(re, sw[0, :, cols]) - dot(im, sw[1, :, cols]),
            dot(re, sw[1, :, cols]) + dot(im, sw[0, :, cols]),
        )
        for r in range(2):
            value = (filtered[r] * gain[:, cols]).astype(bf16)
            back = dot(legp[...], value)
            rsend[ch, :, r * LAT : (r + 1) * LAT, :] = back.astype(bf16).reshape(BAND, LAT, CW)

    def send_c(ch):
        to_rows(ch, lambda row: rsend.at[ch, row], gback.at[ch, my_wavenumber], c_send.at[ch], c_recv.at[ch])

    def by_band(ch):
        wait(gback.at[ch], c_recv.at[ch])

        turned = jnp.swapaxes(gback[ch].astype(f32).reshape(2 * MS, LAT, CW), 0, 1)
        bsend[ch] = turned.astype(bf16)

    def send_d(ch):
        to_bands(lambda q: bsend.at[ch, q], ret.at[ch, lat], d_send.at[ch], d_recv.at[ch])

    def inverse_fourier(ch):
        wait(ret.at[ch], d_recv.at[ch])
        got = ret[ch].astype(f32).reshape(2 * MMAX, CW).astype(bf16)
        ssend[ch] = dot(tabt[...], got).reshape(LON, TILE, CW).astype(bf16)

    def send_e(ch):
        here = tiles.at[row_of(lon, ch), :, pl.ds(ch * CW, CW)]
        to_tiles(lambda n: ssend.at[ch, n], here, e_send.at[ch], e_recv)

    def with_row(ch, step):
        @pl.when(has_row(lon, ch))
        def _():
            step(ch)

    def with_wavenumber(step):
        @pl.when(has_wavenumber(lon))
        def _():
            step()

    load_tab.wait()
    send_legendre()
    for ch in range(CHUNKS):
        with_row(ch, lambda ch: (forward_fourier(ch), send_a(ch)))
    for ch in range(CHUNKS):
        with_row(ch, lambda ch: (by_wavenumber(ch), send_b(ch)))

    load_pleg.wait()
    load_sw.wait()
    load_gain.wait()
    with_wavenumber(order_legendre)

    load_dw.wait()
    load_filt.wait()
    load_offs.wait()
    load_tabt.wait()
    for copy in halo:
        copy.wait_recv()
    stencil()

    @pl.when(has_wavenumber(lon))
    def _():
        for ch in range(CHUNKS):
            legendre(ch)
        for ch in range(CHUNKS):
            mix_and_back(ch)
            send_c(ch)

    for ch in range(CHUNKS):
        with_row(ch, lambda ch: (by_band(ch), send_d(ch)))
    for ch in range(CHUNKS):
        with_row(ch, lambda ch: (inverse_fourier(ch), send_e(ch)))

    wait(tiles, e_recv)

    for copy in halo:
        copy.wait_send()
    for ch in range(CHUNKS):
        mine = has_row(lon, ch)

        @pl.when(mine)
        def _():
            wait(rows.at[ch, pl.ds(0, BAND - 1)], x1_send.at[ch])
            wait(fsend.at[ch, pl.ds(0, LAT - 1)], a_send.at[ch])
            wait(bsend.at[ch, pl.ds(0, LAT - 1)], d_send.at[ch])
            wait(ssend.at[ch, pl.ds(0, LON - 1)], e_send.at[ch])

        @pl.when(jnp.logical_not(mine))
        def _():
            wait(rows.at[ch, pl.ds(0, BAND)], x1_send.at[ch])

        @pl.when(jnp.logical_and(mine, has_wavenumber(lon)))
        def _():
            wait(gsend.at[ch, pl.ds(0, MS - 1)], b_send.at[ch])
            wait(rsend.at[ch, pl.ds(0, BAND - 1)], c_send.at[ch])

        @pl.when(jnp.logical_and(mine, jnp.logical_not(has_wavenumber(lon))))
        def _():
            wait(gsend.at[ch], b_send.at[ch])

        @pl.when(jnp.logical_and(jnp.logical_not(mine), has_wavenumber(lon)))
        def _():
            wait(rsend.at[ch], c_send.at[ch])

    @pl.when(has_wavenumber(lon))
    def _():
        wait(legrecv.at[pl.ds(0, MS - 1)], leg_send)

    @pl.when(jnp.logical_not(has_wavenumber(lon)))
    def _():
        wait(legrecv.at[pl.ds(0, MS)], leg_send)


def on_device(grid_field, disco_filter, offsets, disco_weight, legendre, spec_weight, degree_gain):
    bf16 = jnp.bfloat16
    f32 = jnp.float32
    hbm = pl.BlockSpec(memory_space=pltpu.HBM)
    dma = pltpu.SemaphoreType.DMA
    vmem = pltpu.VMEM
    spectral, disco = pl.pallas_call(
        kernel,
        out_shape=(
            vmem(grid_field.shape, bf16),
            vmem((BAND * TILE, C), f32),
        ),
        in_specs=[hbm] * 10,
        out_specs=(pl.BlockSpec(memory_space=pltpu.VMEM),) * 2,
        scratch_shapes=[
            vmem((BAND, TILE, C), bf16),
            vmem((C // 128, BAND + 4, TILE + 16, 128), f32),
            vmem((KERNELS * C, C), bf16),
            vmem((2, C, C), bf16),
            vmem((LMAX, C), f32),
            vmem((2 * MMAX, NLON), bf16),
            vmem((NLON, 2 * MMAX), bf16),
            vmem((NLAT, NLAT), bf16),
            pltpu.SMEM((5, KERNELS, BAND), f32),
            pltpu.SMEM((5, KERNELS, BAND), jnp.int32),
            vmem((LON, LEG, LMAX), bf16),
            vmem((NLAT, LMAX), bf16),
            vmem((LMAX, NLAT), bf16),
            vmem((CHUNKS, LON, TILE, CW), bf16),
            vmem((CHUNKS, LAT, 2 * MS, CW), bf16),
            vmem((CHUNKS, LAT, 2 * MS, CW), bf16),
            vmem((CHUNKS, MS, 2 * LAT, CW), bf16),
            vmem((CHUNKS, BAND, 2 * LAT, CW), bf16),
            vmem((LMAX, 2 * C), bf16),
            vmem((CHUNKS, BAND, 2 * LAT, CW), bf16),
            vmem((CHUNKS, MS, 2 * LAT, CW), bf16),
            vmem((CHUNKS, LAT, 2 * MS, CW), bf16),
            vmem((CHUNKS, LAT, 2 * MS, CW), bf16),
            vmem((CHUNKS, LON, TILE, CW), bf16),
            vmem((BAND * TILE, KERNELS * C), bf16),
            dma((9,)),
            dma((CHUNKS,)), dma((CHUNKS,)),
            dma, dma,
            dma((8,)), dma((8,)),
            dma((CHUNKS,)), dma((CHUNKS,)),
            dma((CHUNKS,)), dma((CHUNKS,)),
            dma((CHUNKS,)), dma((CHUNKS,)),
            dma((CHUNKS,)), dma((CHUNKS,)),
            dma((CHUNKS,)), dma,
        ],
        compiler_params=pltpu.CompilerParams(
            collective_id=0, has_side_effects=True, vmem_limit_bytes=62 * 1024 * 1024
        ),
        cost_estimate=pl.CostEstimate(flops=3_000_000_000, bytes_accessed=8_000_000, transcendentals=221_184),
    )(
        grid_field,
        jnp.swapaxes(disco_filter, 0, 1),
        jnp.swapaxes(offsets, 0, 1),
        disco_weight.reshape(KERNELS * C, C),
        jnp.swapaxes(legendre.reshape(MS, LMAX, LEG), 1, 2),
        spec_weight,
        degree_gain,
        *constant_tables(),
    )
    combined = spectral.astype(f32) + disco.reshape(grid_field.shape)
    return (grid_field.astype(f32) + jax.nn.gelu(combined)).astype(bf16)


def solution(mesh):
    in_specs = (
        P("lat", "lon", None),
        P(None, None, "lat"),
        P(None, None, "lat"),
        P(),
        P(None, "lat", None, "lon"),
        P(),
        P(),
    )
    out_specs = P("lat", "lon", None)
    return jax.shard_map(
        on_device, mesh=mesh, in_specs=in_specs, out_specs=out_specs, check_vma=False
    )
```

```python
import math

import jax
import jax.numpy as jnp
import numpy as np
from jax import lax
from jax.experimental import pallas as pl
from jax.experimental.pallas import tpu as pltpu
from jax.sharding import PartitionSpec as P

C = 384
NLAT = 384
NLON = 768
MMAX = 384
LMAX = 384
KERNELS = 3
LAT = 32
LON = 16
BAND = NLAT // LAT
TILE = NLON // LON
MS = 12
LEG = NLAT // LON
CHUNKS = 3
CW = C // CHUNKS
MESH = pl.DeviceIdType.MESH


def constant_tables():
    group = np.arange(LAT)[:, None, None, None]
    half = np.arange(2)[None, :, None, None]
    pair = np.arange(6)[None, None, :, None]
    index = group * 6 + pair
    wavenumber = np.where(half == 0, index, MMAX - 1 - index) + np.zeros((1, 1, 1, 2), np.int64)
    component = np.zeros_like(wavenumber) + np.arange(2)
    wavenumber = wavenumber.reshape(-1)
    component = component.reshape(-1)
    phases = (wavenumber[:, None] * np.arange(NLON)[None, :]) % NLON
    angles = phases.astype(np.float32) * np.float32(2.0 * math.pi / NLON)
    values = np.where(component[:, None] == 0, np.cos(angles), -np.sin(angles))
    values = values.astype(np.float32) * np.float32(1.0 / math.sqrt(NLON))
    table = jnp.asarray(values, jnp.bfloat16)
    table_t = jnp.asarray(values.T.copy(), jnp.bfloat16)
    perm_leg = np.zeros((NLAT, NLAT), np.float32)
    for t in range(NLAT):
        perm_leg[(t % BAND) * LAT + t // BAND, t] = 1.0
    return (
        table,
        table_t,
        jnp.asarray(perm_leg, jnp.bfloat16),
    )


def dot(a, b):
    return jnp.dot(a, b, preferred_element_type=jnp.float32)


def kernel(
    grid_hbm, filt_hbm, offs_hbm, dw_hbm, leg_hbm, sw_hbm, gain_hbm, tab_hbm, tabt_hbm, pl_hbm,
    tiles, disco,
    grid_v, pad, dw, sw, gain, tab, tabt, pleg,
    filt, offs, legrecv, legp, legn, rows, fsend, frecv, gsend, hrecv, spec, rsend, gback, bsend, ret, ssend,
    basis,
    load_sem, x1_send, x1_recv, leg_send, leg_recv, halo_send, halo_recv,
    a_send, a_recv, b_send, b_recv, c_send, c_recv, d_send, d_recv, e_send, e_recv,
):
    bf16 = jnp.bfloat16
    f32 = jnp.float32
    lat = lax.axis_index("lat")
    lon = lax.axis_index("lon")
    y = lax.div(lon, 2)
    z = lax.div(lat, 4)
    x = lax.rem(lat, 4)

    def has_row(device, ch):
        return lax.rem(device, 4) != ch

    def row_of(device, ch):
        inner = lax.rem(device, 4)
        return 3 * lax.div(device, 4) + jnp.where(inner > ch, inner - 1, inner)

    def has_wavenumber(device):
        inner = lax.rem(device, 8)
        return jnp.logical_and(inner != 5, inner != 7)

    def wavenumber_of(device):
        return 6 * lax.div(device, 8) + jnp.minimum(lax.rem(device, 8), 5)

    def ring(step):
        near = 4 - lax.div(step + 1, 2)
        return lax.rem(jnp.where(lax.rem(step, 2) == 0, 8 - near, near), 8)

    my_wavenumber = wavenumber_of(lon)

    north = lax.rem(lat + LAT - 1, LAT)
    south = lax.rem(lat + 1, LAT)
    west = lax.rem(lon + LON - 1, LON)
    east = lax.rem(lon + 1, LON)

    loads = [
        pltpu.make_async_copy(src, dst, load_sem.at[n])
        for n, (src, dst) in enumerate(
            (
                (grid_hbm, grid_v), (tab_hbm, tab), (pl_hbm, pleg),
                (dw_hbm, dw), (sw_hbm, sw), (gain_hbm, gain), (tabt_hbm, tabt), (filt_hbm, filt), (offs_hbm, offs),
            )
        )
    ]
    load_grid, load_tab, load_pleg, load_dw, load_sw, load_gain, load_tabt, load_filt, load_offs = loads
    barrier = pltpu.get_barrier_semaphore()

    def greet(device):
        pl.semaphore_signal(barrier, inc=1, device_id=device, device_id_type=MESH)

    for d in range(1, LON):
        greet((lat, lax.rem(lon + d, LON)))
    for d in range(1, LAT):
        greet((lax.rem(lat + d, LAT), lon))

    for a in (north, south):
        for b in (west, east):
            greet((a, b))
    pl.semaphore_wait(barrier, LON - 1 + LAT - 1 + 4)

    def remote(src, dst, send, recv, device):
        return pltpu.make_async_remote_copy(
            src_ref=src, dst_ref=dst, send_sem=send, recv_sem=recv, device_id=device, device_id_type=MESH
        )

    def along_lon(takes, number, source, target, send, recv):
        @pl.loop(0, LON)
        def _(step):
            there = 2 * lax.rem(y + ring(lax.div(step, 2)), 8) + lax.rem(step, 2)
            block = number(there)
            taken = takes(there)

            @pl.when(jnp.logical_and(taken, there != lon))
            def _():
                remote(source(block), target, send, recv, (lat, there)).start()

            @pl.when(jnp.logical_and(taken, there == lon))
            def _():
                pltpu.make_async_copy(source(block), target, recv).start()

    def to_rows(ch, source, target, send, recv):
        along_lon(lambda d: has_row(d, ch), lambda d: row_of(d, ch), source, target, send, recv)

    def to_wavenumbers(source, target, send, recv):
        along_lon(has_wavenumber, wavenumber_of, source, target, send, recv)

    def to_tiles(source, target, send, recv):
        along_lon(lambda d: d >= 0, lambda d: d, source, target, send, recv)

    def to_bands(source, target, send, recv):
        @pl.loop(0, LAT)
        def _(step):
            there = 4 * lax.rem(z + ring(lax.div(step, 4)), 8) + lax.rem(x + 2 + lax.rem(step, 4), 4)

            @pl.when(there != lat)
            def _():
                remote(source(there), target, send, recv, (there, lon)).start()

        pltpu.make_async_copy(source(lat), target, recv).start()

    def wait(ref, sem):
        pltpu.make_async_copy(ref, ref, sem).wait()

    for ch in range(CHUNKS):
        to_rows(
            ch, lambda row: grid_hbm.at[row, :, pl.ds(ch * CW, CW)], rows.at[ch, lon], x1_send.at[ch], x1_recv.at[ch]
        )

    for load in loads:
        load.start()

    load_grid.wait()
    for ct in range(C // 128):
        pad[ct, 2 : 2 + BAND, 8 : 8 + TILE, :] = grid_v[:, :, ct * 128 : (ct + 1) * 128].astype(f32)
    n0, n1 = 8, 8 + TILE
    t0, t1 = 2, 2 + BAND
    halo = [
        remote(
            pad.at[:, pl.ds(sr, nr), pl.ds(sc, nc), :], pad.at[:, pl.ds(dr, nr), pl.ds(dc, nc), :],
            halo_send.at[n], halo_recv.at[n], device,
        )
        for n, (sr, nr, sc, nc, dr, dc, device) in enumerate(
            (
                (t0, BAND, n0, 8, t0, n1, (lat, west)),
                (t0, BAND, n1 - 8, 8, t0, 0, (lat, east)),
                (t0, 2, n0, TILE, t1, n0, (north, lon)),
                (t1 - 2, 2, n0, TILE, 0, n0, (south, lon)),
                (t0, 2, n0, 8, t1, n1, (north, west)),
                (t0, 2, n1 - 8, 8, t1, 0, (north, east)),
                (t1 - 2, 2, n0, 8, 0, n1, (south, west)),
                (t1 - 2, 2, n1 - 8, 8, 0, 0, (south, east)),
            )
        )
    ]
    def send_halo():
        for copy in halo:
            copy.start()

    send_halo()

    def send_legendre():
        to_wavenumbers(lambda m: leg_hbm.at[m], legrecv.at[lon], leg_send, leg_recv)

    def forward_fourier(ch):
        wait(rows.at[ch], x1_recv.at[ch])

        part = dot(tab[...], rows[ch].reshape(NLON, CW))
        fsend[ch] = part.reshape(LAT, 2 * MS, CW).astype(bf16)

    def send_a(ch):
        to_bands(lambda q: fsend.at[ch, q], frecv.at[ch, lat], a_send.at[ch], a_recv.at[ch])

    def order_legendre():
        wait(legrecv, leg_recv)
        shards = legrecv[...].astype(f32).reshape(NLAT, LMAX).astype(bf16)
        ordered = dot(pleg[...], shards)
        legp[...] = ordered.astype(bf16)
        legn[...] = ordered.T.astype(bf16)

    def by_wavenumber(ch):
        wait(frecv.at[ch], a_recv.at[ch])
        turned = jnp.swapaxes(frecv[ch].astype(f32), 0, 1)
        gsend[ch] = turned.reshape(MS, 2 * LAT, CW).astype(bf16)

    def send_b(ch):
        to_wavenumbers(lambda m: gsend.at[ch, m], hrecv.at[ch, row_of(lon, ch)], b_send.at[ch], b_recv.at[ch])

    def stencil():
        @pl.loop(0, BAND)
        def _(i):
            for k in range(KERNELS):
                totals = [jnp.zeros((TILE, 128), f32)] * (C // 128)
                for j in range(5):
                    t = lat * BAND + i + (j - 2)
                    inside = jnp.logical_and(t >= 0, t < NLAT)
                    scale = jnp.where(inside, filt[j, k, i], 0.0)
                    first = 8 + offs[j, k, i]
                    totals = [
                        total + scale * pad[ct, i + j, pl.ds(first, TILE), :] for ct, total in enumerate(totals)
                    ]
                for ct, total in enumerate(totals):
                    at = k * C + ct * 128
                    basis[pl.ds(i * TILE, TILE), at : at + 128] = total.astype(bf16)

        @pl.loop(0, 4)
        def _(b):
            disco[pl.ds(b * 144, 144), :] = dot(basis[pl.ds(b * 144, 144), :], dw[...])

    def legendre(ch):
        wait(hrecv.at[ch], b_recv.at[ch])
        both = jnp.concatenate(
            [hrecv[ch, :, r * LAT : (r + 1) * LAT, :].reshape(NLAT, CW) for r in range(2)], axis=1
        )
        part = dot(legn[...], both).astype(bf16)
        for r in range(2):
            spec[:, r * C + ch * CW : r * C + (ch + 1) * CW] = part[:, r * CW : (r + 1) * CW]

    def mix_and_back(ch):
        cols = slice(ch * CW, (ch + 1) * CW)
        re = spec[:, :C]
        im = spec[:, C:]
        filtered = (
            dot(re, sw[0, :, cols]) - dot(im, sw[1, :, cols]),
            dot(re, sw[1, :, cols]) + dot(im, sw[0, :, cols]),
        )
        values = jnp.concatenate([(part * gain[:, cols]).astype(bf16) for part in filtered], axis=1)
        back = dot(legp[...], values).astype(bf16)
        for r in range(2):
            rsend[ch, :, r * LAT : (r + 1) * LAT, :] = back[:, r * CW : (r + 1) * CW].reshape(BAND, LAT, CW)

    def send_c(ch):
        to_rows(ch, lambda row: rsend.at[ch, row], gback.at[ch, my_wavenumber], c_send.at[ch], c_recv.at[ch])

    def by_band(ch):
        wait(gback.at[ch], c_recv.at[ch])

        turned = jnp.swapaxes(gback[ch].astype(f32).reshape(2 * MS, LAT, CW), 0, 1)
        bsend[ch] = turned.astype(bf16)

    def send_d(ch):
        to_bands(lambda q: bsend.at[ch, q], ret.at[ch, lat], d_send.at[ch], d_recv.at[ch])

    def inverse_fourier(ch):
        wait(ret.at[ch], d_recv.at[ch])
        got = ret[ch].astype(f32).reshape(2 * MMAX, CW).astype(bf16)
        ssend[ch] = dot(tabt[...], got).reshape(LON, TILE, CW).astype(bf16)

    def send_e(ch):
        here = tiles.at[row_of(lon, ch), :, pl.ds(ch * CW, CW)]
        to_tiles(lambda n: ssend.at[ch, n], here, e_send.at[ch], e_recv)

    def with_row(ch, step):
        @pl.when(has_row(lon, ch))
        def _():
            step(ch)

    def with_wavenumber(step):
        @pl.when(has_wavenumber(lon))
        def _():
            step()

    load_tab.wait()
    send_legendre()
    for ch in range(CHUNKS):
        with_row(ch, lambda ch: (forward_fourier(ch), send_a(ch)))
    for ch in range(CHUNKS):
        with_row(ch, lambda ch: (by_wavenumber(ch), send_b(ch)))

    load_pleg.wait()
    load_sw.wait()
    load_gain.wait()
    with_wavenumber(order_legendre)

    load_dw.wait()
    load_filt.wait()
    load_offs.wait()
    load_tabt.wait()
    for copy in halo:
        copy.wait_recv()
    stencil()

    @pl.when(has_wavenumber(lon))
    def _():
        for ch in range(CHUNKS):
            legendre(ch)
        for ch in range(CHUNKS):
            mix_and_back(ch)
            send_c(ch)

    for ch in range(CHUNKS):
        with_row(ch, lambda ch: (by_band(ch), send_d(ch)))
    for ch in range(CHUNKS):
        with_row(ch, lambda ch: (inverse_fourier(ch), send_e(ch)))

    wait(tiles, e_recv)

    for copy in halo:
        copy.wait_send()
    for ch in range(CHUNKS):
        mine = has_row(lon, ch)

        @pl.when(mine)
        def _():
            wait(rows.at[ch, pl.ds(0, BAND - 1)], x1_send.at[ch])
            wait(fsend.at[ch, pl.ds(0, LAT - 1)], a_send.at[ch])
            wait(bsend.at[ch, pl.ds(0, LAT - 1)], d_send.at[ch])
            wait(ssend.at[ch, pl.ds(0, LON - 1)], e_send.at[ch])

        @pl.when(jnp.logical_not(mine))
        def _():
            wait(rows.at[ch, pl.ds(0, BAND)], x1_send.at[ch])

        @pl.when(jnp.logical_and(mine, has_wavenumber(lon)))
        def _():
            wait(gsend.at[ch, pl.ds(0, MS - 1)], b_send.at[ch])
            wait(rsend.at[ch, pl.ds(0, BAND - 1)], c_send.at[ch])

        @pl.when(jnp.logical_and(mine, jnp.logical_not(has_wavenumber(lon))))
        def _():
            wait(gsend.at[ch], b_send.at[ch])

        @pl.when(jnp.logical_and(jnp.logical_not(mine), has_wavenumber(lon)))
        def _():
            wait(rsend.at[ch], c_send.at[ch])

    @pl.when(has_wavenumber(lon))
    def _():
        wait(legrecv.at[pl.ds(0, MS - 1)], leg_send)

    @pl.when(jnp.logical_not(has_wavenumber(lon)))
    def _():
        wait(legrecv.at[pl.ds(0, MS)], leg_send)


def on_device(grid_field, disco_filter, offsets, disco_weight, legendre, spec_weight, degree_gain):
    bf16 = jnp.bfloat16
    f32 = jnp.float32
    hbm = pl.BlockSpec(memory_space=pltpu.HBM)
    dma = pltpu.SemaphoreType.DMA
    vmem = pltpu.VMEM
    spectral, disco = pl.pallas_call(
        kernel,
        out_shape=(
            vmem(grid_field.shape, bf16),
            vmem((BAND * TILE, C), f32),
        ),
        in_specs=[hbm] * 10,
        out_specs=(pl.BlockSpec(memory_space=pltpu.VMEM),) * 2,
        scratch_shapes=[
            vmem((BAND, TILE, C), bf16),
            vmem((C // 128, BAND + 4, TILE + 16, 128), f32),
            vmem((KERNELS * C, C), bf16),
            vmem((2, C, C), bf16),
            vmem((LMAX, C), f32),
            vmem((2 * MMAX, NLON), bf16),
            vmem((NLON, 2 * MMAX), bf16),
            vmem((NLAT, NLAT), bf16),
            pltpu.SMEM((5, KERNELS, BAND), f32),
            pltpu.SMEM((5, KERNELS, BAND), jnp.int32),
            vmem((LON, LEG, LMAX), bf16),
            vmem((NLAT, LMAX), bf16),
            vmem((LMAX, NLAT), bf16),
            vmem((CHUNKS, LON, TILE, CW), bf16),
            vmem((CHUNKS, LAT, 2 * MS, CW), bf16),
            vmem((CHUNKS, LAT, 2 * MS, CW), bf16),
            vmem((CHUNKS, MS, 2 * LAT, CW), bf16),
            vmem((CHUNKS, BAND, 2 * LAT, CW), bf16),
            vmem((LMAX, 2 * C), bf16),
            vmem((CHUNKS, BAND, 2 * LAT, CW), bf16),
            vmem((CHUNKS, MS, 2 * LAT, CW), bf16),
            vmem((CHUNKS, LAT, 2 * MS, CW), bf16),
            vmem((CHUNKS, LAT, 2 * MS, CW), bf16),
            vmem((CHUNKS, LON, TILE, CW), bf16),
            vmem((BAND * TILE, KERNELS * C), bf16),
            dma((9,)),
            dma((CHUNKS,)), dma((CHUNKS,)),
            dma, dma,
            dma((8,)), dma((8,)),
            dma((CHUNKS,)), dma((CHUNKS,)),
            dma((CHUNKS,)), dma((CHUNKS,)),
            dma((CHUNKS,)), dma((CHUNKS,)),
            dma((CHUNKS,)), dma((CHUNKS,)),
            dma((CHUNKS,)), dma,
        ],
        compiler_params=pltpu.CompilerParams(
            collective_id=0, has_side_effects=True, vmem_limit_bytes=62 * 1024 * 1024
        ),
        cost_estimate=pl.CostEstimate(flops=3_000_000_000, bytes_accessed=8_000_000, transcendentals=221_184),
    )(
        grid_field,
        jnp.swapaxes(disco_filter, 0, 1),
        jnp.swapaxes(offsets, 0, 1),
        disco_weight.reshape(KERNELS * C, C),
        jnp.swapaxes(legendre.reshape(MS, LMAX, LEG), 1, 2),
        spec_weight,
        degree_gain,
        *constant_tables(),
    )
    combined = spectral.astype(f32) + disco.reshape(grid_field.shape)
    return (grid_field.astype(f32) + jax.nn.gelu(combined)).astype(bf16)


def solution(mesh):
    in_specs = (
        P("lat", "lon", None),
        P(None, None, "lat"),
        P(None, None, "lat"),
        P(),
        P(None, "lat", None, "lon"),
        P(),
        P(),
    )
    out_specs = P("lat", "lon", None)
    return jax.shard_map(
        on_device, mesh=mesh, in_specs=in_specs, out_specs=out_specs, check_vma=False
    )
```
